32 devices in a mesh: section: 2 (over x), seq: 16 (over z, y, core).
Axes of the slice: x: 2, y: 2, z: 4, core: 2. Of those that a mesh axis runs over, the one named last changes fastest.
Arguments:
- stream: bfloat16 [2, 2048, 4096], P('section', 'seq'), may hold values from -200 to 200
- cotangent: bfloat16 [2, 2048, 4096], P('section', 'seq'), may hold values from -24 to 24
- keys: bfloat16 [2, 2048, 512], P('section', 'seq'), may hold values from -30 to 30
- values: bfloat16 [2, 2048, 512], P('section', 'seq'), may hold values from -6 to 6
- gain: float32 [2, 4096], P('section'), may hold values from 0.5 to 2
- rand_blocks: int32 [16, 1], P('seq'), may hold values from 0 to 15, as said below
Outputs:
- stream_grads: bfloat16 [2, 2048, 4096], P('section', 'seq')
- key_grads: bfloat16 [2, 2048, 512], P('section', 'seq')
- value_grads: bfloat16 [2, 2048, 512], P('section', 'seq')
The draws below stay inside these ranges and needn't reach their ends.
Inputs may be any that keep to these rules, and one draw needn't show every extreme that they name: `rand_blocks`: row d names one block, of the form d xor 2**b with b >= 1; every row d = 2**b with b >= 1 names block 0.
All inputs are finite; a program needn't handle non-finite values.
Results may differ from the reference program's by a relative error of at most 0.012.
The reference program's roundings to bfloat16 on the way count: a program that leaves them out, or rounds other values in their place, can miss the bound.
Values may be sent and summed in bfloat16 or wider, within the bound.
No kernel may reach another device: no remote copies, remote signals or barrier semaphores. Data moves between devices by JAX's collectives and lax.ppermute only.
A program may use at most 128 MiB of HBM per device.

```python
import math
import jax
import jax.numpy as jnp
from jax import lax

QH = 32
HD = 128
BLOCK = 128
RAND = 1
SECTIONS = 2
TOKENS = 2048
NBLK = 16
SLOTS = 5
WIDTH = 4096
KVW = 512


def draw_stream(key, part):
    shape = (SECTIONS, TOKENS, WIDTH)
    return jnp.clip(jax.random.normal(jax.random.fold_in(key, 23), shape), -6.0, 6.0).astype(jnp.bfloat16)


def draw_keys(key, part):
    shape = (SECTIONS, TOKENS, KVW)
    return jnp.clip(2.0 * jax.random.normal(jax.random.fold_in(key, 33), shape), -8.0, 8.0).astype(jnp.bfloat16)


def draw_rand_blocks(key, part):
    block_count = TOKENS // BLOCK
    bit_count = block_count.bit_length() - 1
    row_index = jnp.arange(block_count, dtype=jnp.int32)[:, None]
    bit_values = jnp.arange(1, bit_count, dtype=jnp.int32)[None, :]
    partner = jnp.bitwise_xor(row_index, jnp.left_shift(jnp.int32(1), bit_values))
    noise_draw = jax.random.randint(jax.random.fold_in(key, 41), (block_count, bit_count - 1), 0, 1 << 20)
    ranking = noise_draw * 64 + bit_values
    ranking = jnp.where(partner == 0, 1 << 28, ranking)
    ranked_values, picked = lax.top_k(ranking, RAND)
    chosen_bits = picked.astype(jnp.int32) + 1
    return jnp.bitwise_xor(row_index, jnp.left_shift(jnp.int32(1), chosen_bits)).astype(jnp.int32)


def block_levels(key, extent, split, low, high):
    def one(dim, shards_of):
        steps = jax.random.uniform(jax.random.fold_in(jax.random.fold_in(key, 6), dim), (shards_of,), jnp.float32, low / len(split), high / len(split))
        return jnp.repeat(jnp.exp(steps), extent[dim] // shards_of).reshape((-1,) + (1,) * (len(extent) - dim - 1))

    factor_of = one(*split[0])
    for cut in split[1:]:
        factor_of = factor_of * one(*cut)
    return factor_of


def scatter_about(rng, shape, spread, bound, shards=(), kind=jnp.bfloat16):
    drawn = jax.random.normal(rng, shape, jnp.float32) * spread
    if len(shards) > 0:
        drawn = block_levels(rng, shape, shards, -0.22, 0.18) * drawn
    return jnp.clip(drawn, min=-bound, max=bound).astype(kind)


def setup_inputs(seed: int = 0) -> dict:
    key_list = jax.random.split(jax.random.key(seed), 7)
    stream = draw_stream(jax.random.fold_in(key_list[6], 71), 0)
    cotangent = scatter_about(key_list[1], (SECTIONS, TOKENS, WIDTH), 4.0, 24.0, ((0, 2), (1, 16)))
    keys = draw_keys(jax.random.fold_in(key_list[6], 71), 0)
    values = scatter_about(key_list[3], (SECTIONS, TOKENS, KVW), 1.0, 6.0, ((0, 2), (1, 16)))
    gain = jnp.clip(jnp.exp(math.log(2.0) - 1.3862944 * jax.random.uniform(key_list[4], (SECTIONS, WIDTH), jnp.float32) ** block_levels(key_list[4], (SECTIONS, WIDTH), ((0, 2),), -0.2, 0.2)), 0.5, 2.0)
    rand_blocks = draw_rand_blocks(jax.random.fold_in(key_list[6], 71), 0)
    return dict(stream=stream, cotangent=cotangent, keys=keys, values=values, gain=gain, rand_blocks=rand_blocks)


def rounded(array):
    return lax.optimization_barrier(array.astype(jnp.bfloat16)).astype(jnp.float32)

def group_terms(queries, slot_keys, slot_values, slot_valid, upstream):
    row_count = queries.shape[0]
    head_dim = slot_keys.shape[1]
    head_count = queries.shape[1] // head_dim
    factor = head_dim ** (-0.5)
    best = lax.Precision.HIGHEST
    query_heads = queries.astype(jnp.float32).reshape(row_count, head_count, head_dim)
    grad_heads = upstream.astype(jnp.float32).reshape(row_count, head_count, head_dim)
    key_rows = slot_keys.astype(jnp.float32)
    value_rows = slot_values.astype(jnp.float32)
    scores = jnp.einsum('qhd,kd->hqk', query_heads, key_rows, precision=best) * factor
    scores = jnp.where(slot_valid[None, None, :], scores, -1e+30)
    row_peak = lax.optimization_barrier(jnp.max(scores, axis=2, keepdims=True))
    raised = jnp.exp(scores - row_peak)
    weights = raised / lax.optimization_barrier(jnp.sum(raised, axis=2, keepdims=True))
    weights_low = rounded(weights)
    grad_weights = jnp.einsum('qhd,kd->hqk', grad_heads, value_rows, precision=best)
    centred = grad_weights - lax.optimization_barrier(jnp.sum(weights * grad_weights, axis=2, keepdims=True))
    grad_low = rounded(weights * centred * factor)
    grad_query = jnp.einsum('hqk,kd->qhd', grad_low, key_rows, precision=best)
    grad_keys = jnp.einsum('hqk,qhd->kd', grad_low, query_heads, precision=best)
    grad_values = jnp.einsum('hqk,qhd->kd', weights_low, grad_heads, precision=best)
    return (grad_query.reshape(row_count, head_count * head_dim), grad_keys, grad_values)

def section_terms(hidden, upstream, key_rows, value_rows, gain_row, rand_blocks):
    own = jnp.concatenate([key_rows, value_rows], axis=1).reshape(NBLK, BLOCK, 2 * KVW)
    hidden_wide = hidden.astype(jnp.float32)
    inverse = lax.rsqrt(lax.optimization_barrier(jnp.mean(hidden_wide * hidden_wide, axis=1, keepdims=True)) + 1e-05)
    normed = hidden_wide * inverse
    queries = (normed * gain_row).astype(jnp.bfloat16)
    groups = KVW // HD
    query_cols = QH * HD // groups

    def per_block(index):
        empty = jnp.zeros((BLOCK, 2 * KVW), jnp.bfloat16)
        lower = jnp.maximum(index - 1, 0).astype(jnp.int32)
        upper = jnp.minimum(index + 1, NBLK - 1).astype(jnp.int32)
        parts = [jnp.where(index > 0, own[lower], empty), own[index], jnp.where(index < NBLK - 1, own[upper], empty), own[0]]
        for slot_index in range(RAND):
            parts.append(own[rand_blocks[index, slot_index].astype(jnp.int32)])
        slots = jnp.concatenate(parts, axis=0)
        flags = jnp.stack([index > 0, index >= 0, index < NBLK - 1, index > 0] + [index >= 0] * RAND)
        slot_valid = jnp.repeat(flags, BLOCK)
        start = (index * BLOCK).astype(jnp.int32)
        block_queries = lax.dynamic_slice_in_dim(queries, start, BLOCK, 0)
        block_upstream = lax.dynamic_slice_in_dim(upstream, start, BLOCK, 0)
        query_parts = []
        key_parts = []
        value_parts = []
        for group in range(groups):
            grad_query, grad_keys, grad_values = group_terms(block_queries[:, group * query_cols:(group + 1) * query_cols], slots[:, group * HD:(group + 1) * HD], slots[:, KVW + group * HD:KVW + (group + 1) * HD], slot_valid, block_upstream[:, group * query_cols:(group + 1) * query_cols])
            query_parts.append(grad_query)
            key_parts.append(grad_keys)
            value_parts.append(grad_values)
        grad_slots = jnp.concatenate(key_parts + value_parts, axis=1)
        return (jnp.concatenate(query_parts, axis=1), grad_slots)
    grad_query, grad_slots = lax.map(per_block, jnp.arange(NBLK, dtype=jnp.int32))
    grad_query = grad_query.reshape(TOKENS, QH * HD)
    grad_normed = grad_query * gain_row
    grad_hidden = inverse * (grad_normed - normed * lax.optimization_barrier(jnp.mean(grad_normed * normed, axis=1, keepdims=True)))
    handed = (upstream.astype(jnp.float32) + grad_hidden).astype(jnp.bfloat16)
    terms = grad_slots.reshape(NBLK, SLOTS, BLOCK, 2 * KVW)
    zero_block = jnp.zeros((1, BLOCK, 2 * KVW), jnp.float32)
    from_next = jnp.concatenate([rounded(terms[1:, 0]), zero_block], axis=0)
    from_prev = jnp.concatenate([zero_block, rounded(terms[:-1, 2])], axis=0)
    totals = terms[:, 1] + from_prev + from_next
    random_terms = rounded(terms[:, 4:]).reshape(NBLK * RAND, BLOCK, 2 * KVW)
    totals = totals.at[rand_blocks.reshape(-1).astype(jnp.int32)].add(random_terms)
    totals = totals.at[0].add(lax.optimization_barrier(jnp.sum(terms[:, 3], axis=0)))
    totals = totals.astype(jnp.bfloat16).reshape(TOKENS, 2 * KVW)
    return (handed, totals[:, :KVW], totals[:, KVW:])

def reference(stream, cotangent, keys, values, gain, rand_blocks):

    def per_section(items):
        return section_terms(items[0], items[1], items[2], items[3], items[4], rand_blocks)
    handed, key_grads, value_grads = lax.map(per_section, (stream, cotangent, keys, values, gain))
    return (jnp.roll(handed, -1, axis=0), key_grads, value_grads)
```

```python
import functools
import math

import jax
import jax.numpy as jnp
from jax import lax
from jax.experimental import pallas as pl
from jax.experimental.pallas import tpu as pltpu
from jax.sharding import PartitionSpec as P

HD=128; NT=(((1,),(1,)),((),()))
NN=(((1,),(0,)),((),()))
TN=(((0,),(0,)),((),()))
def dot(a,b,dims): return lax.dot_general(a,b,dims,preferred_element_type=jnp.float32)

def kernel(U, n_partners, heads_per_group, info, stream, cot, gain, own, near, far, glob, *rest):
    partners=rest[:n_partners]
    handed, own_g, near_g, far_g, glob_g = rest[n_partners:n_partners+5]
    partners_g=rest[n_partners+5:2*n_partners+5]
    q, kall, kt, vall, dq, dk, dv = rest[2*n_partners+5:]
    rows, width = stream.shape
    groups=kall.shape[0]
    kvw=groups*HD
    factor=HD**-0.5
    c=factor*math.log2(math.e)
    me, count, want = info[0], info[1], info[2]
    odd = me % 2
    near_at = (1-odd)*2*rows
    far_at = odd*2*rows
    near_at=pl.multiple_of(near_at,rows); far_at=pl.multiple_of(far_at,rows)
    for g in range(groups):
        kc=slice(g*HD,(g+1)*HD); vc=slice(kvw+g*HD,kvw+(g+1)*HD)
        for dst, cols in ((kall,kc),(vall,vc)):
            dst[g, rows:2*rows, :]=own[:,cols]
            dst[g, pl.ds(near_at,rows), :]=near[:,cols]
            dst[g, pl.ds(far_at,rows), :]=far[:,cols]
            dst[g, 3*rows:4*rows, :]=glob[:,cols]
            for b in range(n_partners):
                @pl.when(want == (me ^ (2<<b)))
                def _():
                    dst[g, 4*rows:5*rows, :]=partners[b][:,cols]
        kt[g]=kall[g].astype(jnp.float32).T.astype(jnp.bfloat16)
    CH=512
    ss=jnp.zeros((rows,128),jnp.float32)
    for i in range(width//128):
        x=stream[:,i*128:(i+1)*128].astype(jnp.float32)
        ss=ss+x*x
    inv=lax.rsqrt(jnp.sum(ss,axis=1,keepdims=True)/width+1e-5)
    for i in range(width//CH):
        s=slice(i*CH,(i+1)*CH)
        q[:,s]=(stream[:,s].astype(jnp.float32)*inv*gain[:,s]).astype(jnp.bfloat16)
    dk[...]=jnp.zeros_like(dk); dv[...]=jnp.zeros_like(dv)
    big=jnp.float32(1e30)
    valid=(me>0, None, me<count-1, me>0, None)
    def one(g, off):
        o0=pl.multiple_of(off,2*HD)
        q2=jnp.concatenate([q[:,pl.ds(o0,HD)],q[:,pl.ds(pl.multiple_of(o0+HD,HD),HD)]],axis=0)
        do2=jnp.concatenate([cot[:,pl.ds(o0,HD)],cot[:,pl.ds(pl.multiple_of(o0+HD,HD),HD)]],axis=0)
        s=dot(kall[g],q2,NT)
        gw=dot(vall[g],do2,NT)
        m=None
        for j in range(5):
            mj=jnp.max(s[j*rows:(j+1)*rows],axis=0,keepdims=True)
            if valid[j] is not None: mj=jnp.where(valid[j],mj,-big)
            m = mj if m is None else jnp.maximum(m,mj)
        mc=m*c
        es=[]
        l=0.; t=0.
        for j in range(5):
            mj = mc if valid[j] is None else jnp.where(valid[j],mc,big)
            e=jnp.exp2(s[j*rows:(j+1)*rows]*c-mj)
            l=l+jnp.sum(e,axis=0,keepdims=True)
            t=t+jnp.sum(e*gw[j*rows:(j+1)*rows],axis=0,keepdims=True)
            es.append(e)
        r=1.0/l
        delta=t*r
        e=jnp.concatenate(es,axis=0)
        w=e*r
        wl=w.astype(jnp.bfloat16)
        ds=(w*((gw-delta)*factor)).astype(jnp.bfloat16)
        dv[g]+=dot(wl,do2,NN)
        dk[g]+=dot(ds,q2,NN)
        dqt=dot(kt[g],ds,NN)
        d2=dqt.T
        dq[:,pl.ds(o0,HD)]=d2[:rows]
        dq[:,pl.ds(pl.multiple_of(o0+HD,HD),HD)]=d2[rows:]
    pairs=heads_per_group//2
    per=pairs//U
    def body(i,_):
        g=i//per
        for u in range(U):
            one(g, (i*U+u)*2*HD)
        return 0
    if U==16:
        for i in range(groups*pairs): one(i//pairs, i*2*HD)
    else:
        lax.fori_loop(0,groups*per,body,0)
    for g in range(groups):
        kc=slice(g*HD,(g+1)*HD); vc=slice(kvw+g*HD,kvw+(g+1)*HD)
        for src, cols in ((dk,kc),(dv,vc)):
            own_g[:,cols]=src[g,rows:2*rows]
            near_g[:,cols]=src[g,pl.ds(near_at,rows)].astype(jnp.bfloat16)
            far_g[:,cols]=src[g,pl.ds(far_at,rows)].astype(jnp.bfloat16)
            glob_g[:,cols]=src[g,3*rows:4*rows]
            rt=src[g,4*rows:5*rows].astype(jnp.bfloat16)
            for b in range(n_partners):
                hit=want==(me^(2<<b))
                partners_g[b][:,cols]=jnp.where(hit,rt,jnp.zeros_like(rt))
    acc=jnp.zeros((rows,128),jnp.float32)
    for i in range(width//128):
        s=slice(i*128,(i+1)*128)
        acc=acc+dq[:,s]*gain[:,s]*stream[:,s].astype(jnp.float32)
    mean=jnp.sum(acc,axis=1,keepdims=True)*inv*(1.0/width)
    for i in range(width//CH):
        s=slice(i*CH,(i+1)*CH)
        normed=stream[:,s].astype(jnp.float32)*inv
        gh=inv*(dq[:,s]*gain[:,s]-normed*mean)
        handed[:,s]=(cot[:,s].astype(jnp.float32)+gh).astype(jnp.bfloat16)

def attend(info, stream, cot, gain, own, near, far, glob, partners, U=1):
    rows,width=stream.shape
    kvw=own.shape[1]//2
    groups=kvw//HD
    hpg=width//HD//groups
    npart=len(partners)
    V=pl.BlockSpec(memory_space=pltpu.VMEM)
    blk=jax.ShapeDtypeStruct((rows,2*kvw),jnp.bfloat16)
    blk32=jax.ShapeDtypeStruct((rows,2*kvw),jnp.float32)
    flops=5*2*width*5*rows*rows
    return pl.pallas_call(
        functools.partial(kernel,U,npart,hpg),
        out_shape=[jax.ShapeDtypeStruct((rows,width),jnp.bfloat16),blk32,blk,blk,blk32]+[blk]*npart,
        in_specs=[pl.BlockSpec(memory_space=pltpu.SMEM)]+[V]*(7+npart),
        out_specs=[V]*(5+npart),
        scratch_shapes=[pltpu.VMEM((rows,width),jnp.bfloat16),
            pltpu.VMEM((groups,5*rows,HD),jnp.bfloat16),
            pltpu.VMEM((groups,HD,5*rows),jnp.bfloat16),
            pltpu.VMEM((groups,5*rows,HD),jnp.bfloat16),
            pltpu.VMEM((rows,width),jnp.float32),
            pltpu.VMEM((groups,5*rows,HD),jnp.float32),
            pltpu.VMEM((groups,5*rows,HD),jnp.float32)],
        compiler_params=pltpu.CompilerParams(vmem_limit_bytes=48<<20),
        cost_estimate=pl.CostEstimate(flops=flops,bytes_accessed=8<<20,transcendentals=width*5*rows),
    )(info,stream,cot,gain,own,near,far,glob,*partners)


def permuted(value, pairs, axis="seq"):
    return lax.ppermute(value, axis, pairs)


def global_rounds(count):
    have = [0] + [1 << b for b in range(1, count.bit_length() - 1)]
    missing = [i for i in range(0, count, 2) if i not in have]
    rounds = []
    while missing:
        pairs = []
        for source in sorted(have, reverse=True):
            near = [t for t in missing if t not in [p[1] for p in pairs]]
            if near:
                best = min(near, key=lambda t: (bin(t ^ source).count("1"), abs(t - source)))
                pairs.append((source, best))
        rounds.append(pairs)
        have = have + [t for _, t in pairs]
        missing = [i for i in missing if i not in have]
    return rounds


def among(device, members):
    hit = device == members[0]
    for member in members[1:]:
        hit = hit | (device == member)
    return hit


def on_device(stream, cotangent, keys, values, gain, rand_blocks):
    hidden = stream[0]
    upstream = cotangent[0]
    kv_width = keys.shape[2]
    count = lax.axis_size("seq")
    bits = count.bit_length() - 1
    device = lax.axis_index("seq")
    own = jnp.concatenate([keys[0], values[0]], axis=1)
    swaps = [[(i, i ^ (1 << b)) for i in range(count)] for b in range(bits)]
    across = [(i, i + 1) for i in range(1, count - 1, 2)]
    across = across + [(j, i) for i, j in across]

    partners = [None] * bits
    for b in reversed(range(1, bits)):
        partners[b] = permuted(own, swaps[b])
    far = permuted(own, across)
    near = permuted(own, swaps[0])
    block0 = own
    for b in range(1, bits):
        block0 = jnp.where(device == (1 << b), partners[b], block0)
    for pairs in global_rounds(count):
        got = permuted(block0, pairs)
        block0 = jnp.where(among(device, [t for _, t in pairs]), got, block0)
    got = permuted(block0, [(i, i + 1) for i in range(0, count, 2)])
    block0 = jnp.where(device % 2 == 1, got, block0)

    info = jnp.stack([device, jnp.int32(count), rand_blocks[0, 0]])
    outs = attend(info, hidden, upstream, gain, own, near, far, block0, partners[1:], U=4)
    handed, own_g, near_g, far_g, glob_g = outs[:5]
    partners_g = outs[5:]

    sections = lax.axis_size("section")
    previous = permuted(handed, [((i + 1) % sections, i) for i in range(sections)], "section")
    acc = glob_g
    total = own_g
    for b in range(bits):
        pairs = [(i + (1 << b), i) for i in range(0, count, 2 << b)]
        got = permuted(acc.astype(jnp.bfloat16), pairs)
        acc = acc + got.astype(jnp.float32)
    for b in reversed(range(1, bits)):
        total = total + permuted(partners_g[b - 1], swaps[b]).astype(jnp.float32)
    total = total + permuted(far_g, across).astype(jnp.float32)
    total = total + permuted(near_g, swaps[0]).astype(jnp.float32)
    total = total + jnp.where(device == 0, acc, 0.0)
    total = total.astype(jnp.bfloat16)
    return (previous[None], total[:, :kv_width][None], total[:, kv_width:][None])


def solution(mesh):
    return jax.shard_map(
        on_device,
        mesh=mesh,
        in_specs=(
            P("section", "seq", None),
            P("section", "seq", None),
            P("section", "seq", None),
            P("section", "seq", None),
            P("section", None),
            P("seq", None),
        ),
        out_specs=(P("section", "seq", None), P("section", "seq", None), P("section", "seq", None)),
        check_vma=False,
    )
```

```python
import functools
import math

import jax
import jax.numpy as jnp
from jax import lax
from jax.experimental import pallas as pl
from jax.experimental.pallas import tpu as pltpu
from jax.sharding import PartitionSpec as P

HD = 128
BIG = 1e30
MEGA = 1 << 20
VM_SMALL = 16
VM_ATTEND = 28

NT = (((1,), (1,)), ((), ()))
NN = (((1,), (0,)), ((), ()))


def dot(a, b, dims):
    return lax.dot_general(a, b, dims, preferred_element_type=jnp.float32)


def cost(micros):
    return pl.CostEstimate(flops=int(micros * 1.15e9), bytes_accessed=MEGA, transcendentals=0)


def params(megas):
    return pltpu.CompilerParams(vmem_limit_bytes=megas * MEGA)


VMEM = pl.BlockSpec(memory_space=pltpu.VMEM)
SMEM = pl.BlockSpec(memory_space=pltpu.SMEM)


def prepare_kernel(partner_count, info, stream, gain, own, near, far, *rest):
    partners = rest[:partner_count]
    queries, inverse, slots, key_cols = rest[partner_count:]
    rows, width = stream.shape
    groups = key_cols.shape[0]
    me, want = info[0], info[2]
    odd = me % 2
    near_at = pl.multiple_of((1 - odd) * 2 * rows, rows)
    far_at = pl.multiple_of(odd * 2 * rows, rows)
    slots[rows : 2 * rows, :] = own[...]
    slots[pl.ds(near_at, rows), :] = near[...]
    slots[pl.ds(far_at, rows), :] = far[...]
    slots[3 * rows : 4 * rows, :] = partners[0][...]
    for b in range(1, partner_count):
        @pl.when(want == (me ^ (2 << b)))
        def _():
            slots[3 * rows : 4 * rows, :] = partners[b][...]
    for g in range(groups):
        key_cols[g] = slots[:, g * HD : (g + 1) * HD].T
    squares = jnp.zeros((rows, HD), jnp.float32)
    for i in range(width // HD):
        x = stream[:, i * HD : (i + 1) * HD].astype(jnp.float32)
        squares = squares + x * x
    inv = lax.rsqrt(jnp.sum(squares, axis=1, keepdims=True) / width + 1e-5)
    inv = jnp.broadcast_to(inv, (rows, HD))
    inverse[...] = inv
    for i in range(width // HD):
        s = slice(i * HD, (i + 1) * HD)
        queries[:, s] = (stream[:, s].astype(jnp.float32) * inv * gain[:, s]).astype(jnp.bfloat16)


def prepare(info, stream, gain, own, near, far, partners):
    rows, width = stream.shape
    kvw = own.shape[1] // 2
    groups = kvw // HD
    return pl.pallas_call(
        functools.partial(prepare_kernel, len(partners)),
        out_shape=[
            jax.ShapeDtypeStruct((rows, width), jnp.bfloat16),
            jax.ShapeDtypeStruct((rows, HD), jnp.float32),
            jax.ShapeDtypeStruct((4 * rows, 2 * kvw), jnp.bfloat16),
            jax.ShapeDtypeStruct((groups, HD, 4 * rows), jnp.bfloat16),
        ],
        in_specs=[SMEM] + [VMEM] * (5 + len(partners)),
        out_specs=[VMEM] * 4,
        compiler_params=params(VM_SMALL),
        cost_estimate=cost(6.0),
    )(info, stream, gain, own, near, far, *partners)


def attend_kernel(partner_count, info, stream, cot, gain, queries, inverse, slots, key_cols,
                  even_block, odd_block, *rest):
    handed, own_g, near_g, far_g, glob_g = rest[:5]
    partners_g = rest[5 : 5 + partner_count]
    dq, dk, dv, block, block_t, w0, d0, w1, d1 = rest[5 + partner_count :]
    rows, width = stream.shape
    groups = key_cols.shape[0]
    kvw = groups * HD
    heads = width // HD
    pairs = heads // groups // 2
    count = groups * pairs
    factor = HD**-0.5
    scale = factor * math.log2(math.e)
    me, devices, want = info[0], info[1], info[2]
    odd = me % 2
    valid = (me > 0, None, me < devices - 1, None, me > 0)
    block[...] = jnp.where(odd == 1, odd_block[...], even_block[...])
    for g in range(groups):
        block_t[g] = block[:, g * HD : (g + 1) * HD].T

    def stack(ref, i):
        at = 2 * i * HD
        return jnp.concatenate([ref[:, at : at + HD], ref[:, at + HD : at + 2 * HD]], axis=0)

    def weigh(i, low, grad):
        g = i // pairs
        kc = slice(g * HD, (g + 1) * HD)
        vc = slice(kvw + g * HD, kvw + (g + 1) * HD)
        q2, do2 = stack(queries, i), stack(cot, i)
        s4, g4 = dot(slots[:, kc], q2, NT), dot(slots[:, vc], do2, NT)
        s1, g1 = dot(block[:, kc], q2, NT), dot(block[:, vc], do2, NT)
        scores = [s4[j * rows : (j + 1) * rows] for j in range(4)] + [s1]
        gws = [g4[j * rows : (j + 1) * rows] for j in range(4)] + [g1]
        peak = jnp.max(scores[1], axis=0, keepdims=True)
        for j in (0, 2, 3, 4):
            top = jnp.max(scores[j], axis=0, keepdims=True)
            if valid[j] is not None:
                top = jnp.where(valid[j], top, -BIG)
            peak = jnp.maximum(peak, top)
        peak = peak * scale
        raised = []
        total = 0.0
        weighted = 0.0
        for j in range(5):
            shift = peak if valid[j] is None else jnp.where(valid[j], peak, BIG)
            e = jnp.exp2(scores[j] * scale - shift)
            total = total + jnp.sum(e, axis=0, keepdims=True)
            weighted = weighted + jnp.sum(e * gws[j], axis=0, keepdims=True)
            raised.append(e)
        share = 1.0 / total
        centre = weighted * share
        for j in range(5):
            w = raised[j] * share
            low[j * rows : (j + 1) * rows] = w.astype(jnp.bfloat16)
            grad[j * rows : (j + 1) * rows] = (w * ((gws[j] - centre) * factor)).astype(jnp.bfloat16)

    def spread(i, low, grad):
        g = i // pairs
        q2, do2 = stack(queries, i), stack(cot, i)
        value_part = dot(low[...], do2, NN)
        key_part = dot(grad[...], q2, NN)
        if i % pairs == 0:
            dv[g] = value_part
            dk[g] = key_part
        else:
            dv[g] += value_part
            dk[g] += key_part
        cols = dot(key_cols[g], grad[: 4 * rows], NN) + dot(block_t[g], grad[4 * rows :], NN)
        back = cols.T
        at = 2 * i * HD
        dq[:, at : at + HD] = back[:rows]
        dq[:, at + HD : at + 2 * HD] = back[rows:]

    buffers = ((w0, d0), (w1, d1))
    weigh(0, *buffers[0])
    for i in range(1, count):
        weigh(i, *buffers[i % 2])
        spread(i - 1, *buffers[(i - 1) % 2])
    spread(count - 1, *buffers[(count - 1) % 2])

    inv = inverse[...]
    products = jnp.zeros((rows, HD), jnp.float32)
    for i in range(width // HD):
        s = slice(i * HD, (i + 1) * HD)
        products = products + dq[:, s] * gain[:, s] * stream[:, s].astype(jnp.float32)
    mean = jnp.sum(products, axis=1, keepdims=True) * (1.0 / width) * inv
    pull = inv * inv * mean
    for i in range(width // HD):
        s = slice(i * HD, (i + 1) * HD)
        x = stream[:, s].astype(jnp.float32)
        grad_hidden = dq[:, s] * gain[:, s] * inv - x * pull
        handed[:, s] = (cot[:, s].astype(jnp.float32) + grad_hidden).astype(jnp.bfloat16)

    near_at = pl.multiple_of((1 - odd) * 2 * rows, rows)
    far_at = pl.multiple_of(odd * 2 * rows, rows)
    for g in range(groups):
        kc = slice(g * HD, (g + 1) * HD)
        vc = slice(kvw + g * HD, kvw + (g + 1) * HD)
        for source, cols in ((dk, kc), (dv, vc)):
            own_g[:, cols] = source[g, rows : 2 * rows]
            near_g[:, cols] = source[g, pl.ds(near_at, rows)].astype(jnp.bfloat16)
            far_g[:, cols] = source[g, pl.ds(far_at, rows)].astype(jnp.bfloat16)
            glob_g[:, cols] = source[g, 4 * rows : 5 * rows]
            term = source[g, 3 * rows : 4 * rows].astype(jnp.bfloat16)
            for b in range(partner_count):
                hit = want == (me ^ (2 << b))
                partners_g[b][:, cols] = jnp.where(hit, term, jnp.zeros_like(term))


def attend(info, stream, cot, gain, queries, inverse, slots, key_cols, even_block, odd_block, partner_count):
    rows, width = stream.shape
    groups = key_cols.shape[0]
    kvw = groups * HD
    low = jax.ShapeDtypeStruct((rows, 2 * kvw), jnp.bfloat16)
    wide = jax.ShapeDtypeStruct((rows, 2 * kvw), jnp.float32)
    return pl.pallas_call(
        functools.partial(attend_kernel, partner_count),
        out_shape=[jax.ShapeDtypeStruct((rows, width), jnp.bfloat16), wide, low, low, wide] + [low] * partner_count,
        in_specs=[SMEM] + [VMEM] * 9,
        out_specs=[VMEM] * (5 + partner_count),
        scratch_shapes=[
            pltpu.VMEM((rows, width), jnp.float32),
            pltpu.VMEM((groups, 5 * rows, HD), jnp.float32),
            pltpu.VMEM((groups, 5 * rows, HD), jnp.float32),
            pltpu.VMEM((rows, 2 * kvw), jnp.bfloat16),
            pltpu.VMEM((groups, HD, rows), jnp.bfloat16),
        ]
        + [pltpu.VMEM((5 * rows, 2 * rows), jnp.bfloat16)] * 4,
        compiler_params=params(VM_ATTEND),
        cost_estimate=cost(12.0),
    )(info, stream, cot, gain, queries, inverse, slots, key_cols, even_block, odd_block)


def collect_kernel(own, *rest):
    total = own[...]
    for ref in rest[:-1]:
        total = total + ref[...].astype(jnp.float32)
    rest[-1][...] = total


def collect(own, parts):
    return pl.pallas_call(
        collect_kernel,
        out_shape=jax.ShapeDtypeStruct(own.shape, jnp.float32),
        in_specs=[VMEM] * (1 + len(parts)),
        out_specs=VMEM,
        compiler_params=params(VM_SMALL),
        cost_estimate=cost(0.5),
    )(own, *parts)


def land_kernel(source, target):
    target[...] = source[...]


def land(rows):
    return pl.pallas_call(
        land_kernel,
        out_shape=jax.ShapeDtypeStruct(rows.shape, rows.dtype),
        in_specs=[VMEM],
        out_specs=VMEM,
        compiler_params=params(VM_SMALL),
        cost_estimate=cost(1.0),
    )(rows)


def finish_kernel(info, total, acc, got, keys, values):
    kvw = keys.shape[1]
    last = acc[...] + got[...].astype(jnp.float32)
    result = (total[...] + jnp.where(info[0] == 0, last, 0.0)).astype(jnp.bfloat16)
    keys[...] = result[:, :kvw]
    values[...] = result[:, kvw:]


def finish(info, total, acc, got):
    half = jax.ShapeDtypeStruct((total.shape[0], total.shape[1] // 2), jnp.bfloat16)
    return pl.pallas_call(
        finish_kernel,
        out_shape=[half, half],
        in_specs=[SMEM] + [VMEM] * 3,
        out_specs=[VMEM] * 2,
        compiler_params=params(VM_SMALL),
        cost_estimate=cost(0.5),
    )(info, total, acc, got)


def permuted(value, pairs, axis="seq"):
    return lax.ppermute(value, axis, pairs)


def global_rounds(count, have):
    missing = [i for i in range(0, count, 2) if i not in have]
    rounds = []
    while missing:
        pairs = []
        for source in sorted(have, reverse=True):
            free = [t for t in missing if t not in [p[1] for p in pairs]]
            if free:
                best = min(free, key=lambda t: (bin(t ^ source).count("1"), abs(t - source)))
                pairs.append((source, best))
        rounds.append(pairs)
        have = have + [t for _, t in pairs]
        missing = [i for i in missing if i not in have]
    return rounds


def among(device, members):
    hit = device == members[0]
    for member in members[1:]:
        hit = hit | (device == member)
    return hit


def on_device(stream, cotangent, keys, values, gain, rand_blocks):
    hidden = stream[0]
    upstream = cotangent[0]
    count = lax.axis_size("seq")
    bits = count.bit_length() - 1
    device = lax.axis_index("seq")
    own = jnp.concatenate([keys[0], values[0]], axis=1)
    swaps = [[(i, i ^ (1 << b)) for i in range(count)] for b in range(bits)]
    across = [(i, i + 1) for i in range(1, count - 1, 2)]
    across = across + [(j, i) for i, j in across]
    info = jnp.stack([device, jnp.int32(count), rand_blocks[0, 0]])

    top = count // 4 * 3
    partners = [None] * bits
    for b in reversed(range(2, bits)):
        partners[b] = permuted(own, swaps[b])
    block_top = permuted(own, [(0, top)])
    partners[1] = permuted(own, swaps[1])
    far = permuted(own, across)
    near = permuted(own, swaps[0])

    block0 = jnp.where(device == top, block_top, own)
    for b in range(1, bits):
        block0 = jnp.where(device == (1 << b), partners[b], block0)
    block0, far = lax.optimization_barrier((block0, far))
    for pairs in global_rounds(count, [0, top] + [1 << b for b in range(1, bits)]):
        moved = permuted(block0, pairs)
        block0 = jnp.where(among(device, [t for _, t in pairs]), moved, block0)
    odd_block = permuted(block0, [(i, i + 1) for i in range(0, count, 2)])
    queries, inverse, slots, key_cols = prepare(info, hidden, gain, own, near, far, partners[1:])
    outs = attend(info, hidden, upstream, gain, queries, inverse, slots, key_cols, block0, odd_block, bits - 1)
    handed, own_g, near_g, far_g, glob_g = outs[:5]
    partners_g = outs[5:]

    sections = lax.axis_size("section")
    back = [((i + 1) % sections, i) for i in range(sections)]
    previous = land(permuted(handed, back, "section"))
    parts = [permuted(near_g, swaps[0]), permuted(far_g, across)]
    parts = parts + [permuted(partners_g[b - 1], swaps[b]) for b in range(1, bits)]
    acc = glob_g
    for b in range(bits):
        pairs = [(i + (1 << b), i) for i in range(0, count, 2 << b)]
        last = permuted(acc.astype(jnp.bfloat16), pairs)
        if b < bits - 1:
            acc = acc + last.astype(jnp.float32)
    total = collect(own_g, parts)
    key_grads, value_grads = finish(info, total, acc, last)
    return (previous[None], key_grads[None], value_grads[None])


def solution(mesh):
    return jax.shard_map(
        on_device,
        mesh=mesh,
        in_specs=(
            P("section", "seq", None),
            P("section", "seq", None),
            P("section", "seq", None),
            P("section", "seq", None),
            P("section", None),
            P("seq", None),
        ),
        out_specs=(P("section", "seq", None), P("section", "seq", None), P("section", "seq", None)),
        check_vma=False,
    )
```

```python
import functools
import math

import jax
import jax.numpy as jnp
from jax import lax
from jax.experimental import pallas as pl
from jax.experimental.pallas import tpu as pltpu
from jax.sharding import PartitionSpec as P

HD = 128
BIG = 1e30
MEGA = 1 << 20
VM_SMALL = 8
VM_ATTEND = 20

NT = (((1,), (1,)), ((), ()))
NN = (((1,), (0,)), ((), ()))


def dot(a, b, dims):
    return lax.dot_general(a, b, dims, preferred_element_type=jnp.float32)


def cost(micros):
    return pl.CostEstimate(flops=int(micros * 1.15e9), bytes_accessed=MEGA, transcendentals=0)


def params(megas):
    return pltpu.CompilerParams(vmem_limit_bytes=megas * MEGA)


VMEM = pl.BlockSpec(memory_space=pltpu.VMEM)
SMEM = pl.BlockSpec(memory_space=pltpu.SMEM)


def prepare_kernel(partner_count, info, stream, gain, own, near, far, *rest):
    partners = rest[:partner_count]
    queries, inverse, slots, key_cols = rest[partner_count:]
    rows, width = stream.shape
    groups = key_cols.shape[0]
    me, want = info[0], info[2]
    odd = me % 2
    near_at = pl.multiple_of((1 - odd) * 2 * rows, rows)
    far_at = pl.multiple_of(odd * 2 * rows, rows)
    slots[rows : 2 * rows, :] = own[...]
    slots[pl.ds(near_at, rows), :] = near[...]
    slots[pl.ds(far_at, rows), :] = far[...]
    slots[3 * rows : 4 * rows, :] = partners[0][...]
    for b in range(1, partner_count):
        @pl.when(want == (me ^ (2 << b)))
        def _():
            slots[3 * rows : 4 * rows, :] = partners[b][...]
    for g in range(groups):
        key_cols[g] = slots[:, g * HD : (g + 1) * HD].T
    squares = jnp.zeros((rows, HD), jnp.float32)
    for i in range(width // HD):
        x = stream[:, i * HD : (i + 1) * HD].astype(jnp.float32)
        squares = squares + x * x
    inv = lax.rsqrt(jnp.sum(squares, axis=1, keepdims=True) / width + 1e-5)
    inv = jnp.broadcast_to(inv, (rows, HD))
    inverse[...] = inv
    for i in range(width // HD):
        s = slice(i * HD, (i + 1) * HD)
        queries[:, s] = (stream[:, s].astype(jnp.float32) * inv * gain[:, s]).astype(jnp.bfloat16)


def prepare(info, stream, gain, own, near, far, partners):
    rows, width = stream.shape
    kvw = own.shape[1] // 2
    groups = kvw // HD
    return pl.pallas_call(
        functools.partial(prepare_kernel, len(partners)),
        out_shape=[
            jax.ShapeDtypeStruct((rows, width), jnp.bfloat16),
            jax.ShapeDtypeStruct((rows, HD), jnp.float32),
            jax.ShapeDtypeStruct((4 * rows, 2 * kvw), jnp.bfloat16),
            jax.ShapeDtypeStruct((groups, HD, 4 * rows), jnp.bfloat16),
        ],
        in_specs=[SMEM] + [VMEM] * (5 + len(partners)),
        out_specs=[VMEM] * 4,
        compiler_params=params(VM_SMALL),
        cost_estimate=cost(6.0),
    )(info, stream, gain, own, near, far, *partners)


def attend_kernel(partner_count, info, stream, cot, gain, queries, inverse, slots, key_cols,
                  even_block, odd_block, *rest):
    handed, own_g, near_g, far_g, keep_g, across_g, corner_g = rest[:7]
    partners_g = rest[7 : 7 + partner_count]
    dq, products, dk, dv, block, block_t, w0, d0, w1, d1 = rest[7 + partner_count :]
    rows, width = stream.shape
    groups = key_cols.shape[0]
    kvw = groups * HD
    heads = width // HD
    pairs = heads // groups // 2
    count = groups * pairs
    factor = HD**-0.5
    scale = factor * math.log2(math.e)
    me, devices, want = info[0], info[1], info[2]
    odd = me % 2
    valid = (me > 0, None, me < devices - 1, None, me > 0)
    block[...] = jnp.where(odd == 1, odd_block[...], even_block[...])
    for g in range(groups):
        block_t[g] = block[:, g * HD : (g + 1) * HD].T

    def stack(ref, i):
        at = 2 * i * HD
        return jnp.concatenate([ref[:, at : at + HD], ref[:, at + HD : at + 2 * HD]], axis=0)

    def weigh(i, low, grad):
        g = i // pairs
        kc = slice(g * HD, (g + 1) * HD)
        vc = slice(kvw + g * HD, kvw + (g + 1) * HD)
        q2, do2 = stack(queries, i), stack(cot, i)
        s4, g4 = dot(slots[:, kc], q2, NT), dot(slots[:, vc], do2, NT)
        s1, g1 = dot(block[:, kc], q2, NT), dot(block[:, vc], do2, NT)
        scores = [s4[j * rows : (j + 1) * rows] for j in range(4)] + [s1]
        gws = [g4[j * rows : (j + 1) * rows] for j in range(4)] + [g1]
        peak = jnp.max(scores[1], axis=0, keepdims=True)
        for j in (0, 2, 3, 4):
            top = jnp.max(scores[j], axis=0, keepdims=True)
            if valid[j] is not None:
                top = jnp.where(valid[j], top, -BIG)
            peak = jnp.maximum(peak, top)
        peak = peak * scale
        raised = []
        total = 0.0
        weighted = 0.0
        for j in range(5):
            shift = peak if valid[j] is None else jnp.where(valid[j], peak, BIG)
            e = jnp.exp2(scores[j] * scale - shift)
            total = total + jnp.sum(e, axis=0, keepdims=True)
            weighted = weighted + jnp.sum(e * gws[j], axis=0, keepdims=True)
            raised.append(e)
        share = 1.0 / total
        centre = weighted * share
        for j in range(5):
            w = raised[j] * share
            low[j * rows : (j + 1) * rows] = w.astype(jnp.bfloat16)
            grad[j * rows : (j + 1) * rows] = (w * (gws[j] - centre)).astype(jnp.bfloat16)

    def spread(i, low, grad):
        g = i // pairs
        q2, do2 = stack(queries, i), stack(cot, i)
        value_part = dot(low[...], do2, NN)
        key_part = dot(grad[...], q2, NN)
        if i % pairs == 0:
            dv[g] = value_part
            dk[g] = key_part
        else:
            dv[g] += value_part
            dk[g] += key_part
        cols = dot(key_cols[g], grad[: 4 * rows], NN) + dot(block_t[g], grad[4 * rows :], NN)
        back = cols.T
        for h in range(2):
            s = slice((2 * i + h) * HD, (2 * i + h + 1) * HD)
            part = back[h * rows : (h + 1) * rows] * (gain[:, s] * factor)
            dq[:, s] = part
            products[...] += part * stream[:, s].astype(jnp.float32)

    products[...] = jnp.zeros_like(products)
    buffers = ((w0, d0), (w1, d1))
    weigh(0, *buffers[0])
    for i in range(1, count):
        weigh(i, *buffers[i % 2])
        spread(i - 1, *buffers[(i - 1) % 2])
    spread(count - 1, *buffers[(count - 1) % 2])

    inv = inverse[...]
    mean = jnp.sum(products[...], axis=1, keepdims=True) * (1.0 / width) * inv
    pull = inv * inv * mean
    for i in range(width // HD):
        s = slice(i * HD, (i + 1) * HD)
        x = stream[:, s].astype(jnp.float32)
        grad_hidden = dq[:, s] * inv - x * pull
        handed[:, s] = (cot[:, s].astype(jnp.float32) + grad_hidden).astype(jnp.bfloat16)

    share = rows // 4

    def share_at(mask):
        return pl.multiple_of(4 * rows + ((me % 4) ^ mask) * share, share)

    near_at = pl.multiple_of((1 - odd) * 2 * rows, rows)
    far_at = pl.multiple_of(odd * 2 * rows, rows)
    for g in range(groups):
        kc = slice(g * HD, (g + 1) * HD)
        vc = slice(kvw + g * HD, kvw + (g + 1) * HD)
        dk[g] = dk[g] * factor
        for source, cols in ((dk, kc), (dv, vc)):
            own_g[:, cols] = source[g, rows : 2 * rows]
            near_g[:rows, cols] = source[g, pl.ds(near_at, rows)].astype(jnp.bfloat16)
            far_g[:, cols] = source[g, pl.ds(far_at, rows)].astype(jnp.bfloat16)
            keep_g[:, cols] = source[g, pl.ds(share_at(0), share)]
            near_g[rows:, cols] = source[g, pl.ds(share_at(1), share)].astype(jnp.bfloat16)
            across_g[:, cols] = source[g, pl.ds(share_at(2), share)].astype(jnp.bfloat16)
            corner_g[:, cols] = source[g, pl.ds(share_at(3), share)].astype(jnp.bfloat16)
            term = source[g, 3 * rows : 4 * rows].astype(jnp.bfloat16)
            for b in range(partner_count):
                hit = want == (me ^ (2 << b))
                partners_g[b][:, cols] = jnp.where(hit, term, jnp.zeros_like(term))


def attend(info, stream, cot, gain, queries, inverse, slots, key_cols, even_block, odd_block, partner_count):
    rows, width = stream.shape
    groups = key_cols.shape[0]
    kvw = groups * HD
    low = jax.ShapeDtypeStruct((rows, 2 * kvw), jnp.bfloat16)
    wide = jax.ShapeDtypeStruct((rows, 2 * kvw), jnp.float32)
    longer = jax.ShapeDtypeStruct((rows + rows // 4, 2 * kvw), jnp.bfloat16)
    kept = jax.ShapeDtypeStruct((rows // 4, 2 * kvw), jnp.float32)
    share = jax.ShapeDtypeStruct((rows // 4, 2 * kvw), jnp.bfloat16)
    return pl.pallas_call(
        functools.partial(attend_kernel, partner_count),
        out_shape=[jax.ShapeDtypeStruct((rows, width), jnp.bfloat16), wide, longer, low, kept, share, share] + [low] * partner_count,
        in_specs=[SMEM] + [VMEM] * 9,
        out_specs=[VMEM] * (7 + partner_count),
        scratch_shapes=[
            pltpu.VMEM((rows, width), jnp.float32),
            pltpu.VMEM((rows, HD), jnp.float32),
            pltpu.VMEM((groups, 5 * rows, HD), jnp.float32),
            pltpu.VMEM((groups, 5 * rows, HD), jnp.float32),
            pltpu.VMEM((rows, 2 * kvw), jnp.bfloat16),
            pltpu.VMEM((groups, HD, rows), jnp.bfloat16),
        ]
        + [pltpu.VMEM((5 * rows, 2 * rows), jnp.bfloat16)] * 4,
        compiler_params=params(VM_ATTEND),
        cost_estimate=cost(12.0),
    )(info, stream, cot, gain, queries, inverse, slots, key_cols, even_block, odd_block)


def collect_kernel(own, *rest):
    total = own[...]
    for ref in rest[:-1]:
        total = total + ref[: own.shape[0], :].astype(jnp.float32)
    rest[-1][...] = total


def collect(own, parts):
    return pl.pallas_call(
        collect_kernel,
        out_shape=jax.ShapeDtypeStruct(own.shape, jnp.float32),
        in_specs=[VMEM] * (1 + len(parts)),
        out_specs=VMEM,
        compiler_params=params(VM_SMALL),
        cost_estimate=cost(0.5),
    )(own, *parts)


def finish_kernel(info, total, received, acc, *rest):
    previous, keys, values = rest[-3:]
    others = rest[-6:-3]
    previous[...] = received[...]
    kvw = keys.shape[1]
    rows = acc.shape[0]
    first = info[0] == 0
    last = acc[...]
    for ref in rest[:-6]:
        last = last + ref[...].astype(jnp.float32)
    for k in range(4):
        part = last if k == 0 else others[k - 1][...].astype(jnp.float32)
        part = jnp.where(first, part, 0.0)
        result = (total[k * rows : (k + 1) * rows, :] + part).astype(jnp.bfloat16)
        keys[k * rows : (k + 1) * rows, :] = result[:, :kvw]
        values[k * rows : (k + 1) * rows, :] = result[:, kvw:]


def finish(info, total, received, acc, terms, others):
    shape = jax.ShapeDtypeStruct((total.shape[0], total.shape[1] // 2), jnp.bfloat16)
    return pl.pallas_call(
        finish_kernel,
        out_shape=[jax.ShapeDtypeStruct(received.shape, received.dtype), shape, shape],
        in_specs=[SMEM] + [VMEM] * (3 + len(terms) + len(others)),
        out_specs=[VMEM] * 3,
        compiler_params=params(VM_SMALL),
        cost_estimate=cost(0.5),
    )(info, total, received, acc, *terms, *others)


def permuted(value, pairs, axis="seq"):
    return lax.ppermute(value, axis, pairs)


def global_rounds(count, have):
    missing = [i for i in range(0, count, 2) if i not in have]
    rounds = []
    while missing:
        pairs = []
        for source in sorted(have, reverse=True):
            free = [t for t in missing if t not in [p[1] for p in pairs]]
            if free:
                best = min(free, key=lambda t: (bin(t ^ source).count("1"), abs(t - source)))
                pairs.append((source, best))
        rounds.append(pairs)
        have = have + [t for _, t in pairs]
        missing = [i for i in missing if i not in have]
    return rounds


def among(device, members):
    hit = device == members[0]
    for member in members[1:]:
        hit = hit | (device == member)
    return hit


def on_device(stream, cotangent, keys, values, gain, rand_blocks):
    hidden = stream[0]
    upstream = cotangent[0]
    count = lax.axis_size("seq")
    bits = count.bit_length() - 1
    device = lax.axis_index("seq")
    own = jnp.concatenate([keys[0], values[0]], axis=1)
    swaps = [[(i, i ^ (1 << b)) for i in range(count)] for b in range(bits)]
    across = [(i, i + 1) for i in range(1, count - 1, 2)]
    across = across + [(j, i) for i, j in across]
    info = jnp.stack([device, jnp.int32(count), rand_blocks[0, 0]])

    top = count // 4 * 3
    partners = [None] * bits
    for b in reversed(range(2, bits)):
        partners[b] = permuted(own, swaps[b])
    block_top = permuted(own, [(0, top)])
    partners[1] = permuted(own, swaps[1])
    far = permuted(own, across)
    near = permuted(own, swaps[0])

    block0 = jnp.where(device == top, block_top, own)
    for b in range(1, bits):
        block0 = jnp.where(device == (1 << b), partners[b], block0)
    block0, far = lax.optimization_barrier((block0, far))
    for pairs in global_rounds(count, [0, top] + [1 << b for b in range(1, bits)]):
        masks = {i ^ j for i, j in pairs}
        if len(masks) == 1:
            route = swaps[masks.pop().bit_length() - 1]
        else:
            route = pairs
        moved = permuted(block0, route)
        block0 = jnp.where(among(device, [t for _, t in pairs]), moved, block0)
    odd_block = permuted(block0, swaps[0])
    queries, inverse, slots, key_cols = prepare(info, hidden, gain, own, near, far, partners[1:])
    outs = attend(info, hidden, upstream, gain, queries, inverse, slots, key_cols, block0, odd_block, bits - 1)
    handed, own_g, near_g, far_g, keep_g, across_g, corner_g = outs[:7]
    partners_g = outs[7:]

    sections = lax.axis_size("section")
    back = [((i + 1) % sections, i) for i in range(sections)]
    rows = own.shape[0]

    def swapped(value, mask):
        return permuted(value, [(i, i ^ mask) for i in range(count)])

    received = permuted(handed, back, "section")
    near_r = permuted(near_g, swaps[0])
    parts = [near_r, permuted(partners_g[0], swaps[1])]
    for b in reversed(range(2, bits)):
        parts.append(permuted(partners_g[b - 1], swaps[b]))
    parts.append(permuted(far_g, across))

    terms = [near_r[rows:], swapped(across_g, 2), swapped(corner_g, 3)]
    acc = keep_g
    for b in range(2, bits, 2):
        acc = acc + sum(t.astype(jnp.float32) for t in terms)
        low = acc.astype(jnp.bfloat16)
        terms = [swapped(low, k << b) for k in range(1, 1 << min(2, bits - b))]
    mine = (acc + sum(t.astype(jnp.float32) for t in terms)).astype(jnp.bfloat16)
    others = [swapped(mine, mask) for mask in (1, 2, 3)]
    total = collect(own_g, parts)
    previous, key_grads, value_grads = finish(info, total, received, acc, terms, others)
    return (previous[None], key_grads[None], value_grads[None])


def solution(mesh):
    return jax.shard_map(
        on_device,
        mesh=mesh,
        in_specs=(
            P("section", "seq", None),
            P("section", "seq", None),
            P("section", "seq", None),
            P("section", "seq", None),
            P("section", None),
            P("seq", None),
        ),
        out_specs=(P("section", "seq", None), P("section", "seq", None), P("section", "seq", None)),
        check_vma=False,
    )
```

```python
import functools
import math

import jax
import jax.numpy as jnp
from jax import lax
from jax.experimental import pallas as pl
from jax.experimental.pallas import tpu as pltpu
from jax.sharding import PartitionSpec as P

HD = 128
BIG = 1e30
MEGA = 1 << 20
VM_SMALL = 6
VM_LOCAL = 6
VM_TERMS = 6
VM_ATTEND = 8

NT = (((1,), (1,)), ((), ()))
NN = (((1,), (0,)), ((), ()))


def dot(a, b, dims):
    return lax.dot_general(a, b, dims, preferred_element_type=jnp.float32)


def cost(micros):
    return pl.CostEstimate(flops=int(micros * 1.15e9), bytes_accessed=MEGA, transcendentals=0)


def params(megas):
    return pltpu.CompilerParams(vmem_limit_bytes=megas * MEGA)


VMEM = pl.BlockSpec(memory_space=pltpu.VMEM)
SMEM = pl.BlockSpec(memory_space=pltpu.SMEM)


def prepare_kernel(partner_count, info, stream, gain, own, near, far, *rest):
    partners = rest[:partner_count]
    queries, inverse, slots, key_cols = rest[partner_count:]
    rows, width = stream.shape
    groups = key_cols.shape[0]
    me, want = info[0], info[2]
    odd = me % 2
    near_at = pl.multiple_of((1 - odd) * 2 * rows, rows)
    far_at = pl.multiple_of(odd * 2 * rows, rows)
    slots[rows : 2 * rows, :] = own[...]
    slots[pl.ds(near_at, rows), :] = near[...]
    slots[pl.ds(far_at, rows), :] = far[...]
    slots[3 * rows : 4 * rows, :] = partners[0][...]
    for b in range(1, partner_count):
        @pl.when(want == (me ^ (2 << b)))
        def _():
            slots[3 * rows : 4 * rows, :] = partners[b][...]
    for g in range(groups):
        key_cols[g] = slots[:, g * HD : (g + 1) * HD].T
    squares = jnp.zeros((rows, HD), jnp.float32)
    for i in range(width // HD):
        x = stream[:, i * HD : (i + 1) * HD].astype(jnp.float32)
        squares = squares + x * x
    inv = lax.rsqrt(jnp.sum(squares, axis=1, keepdims=True) / width + 1e-5)
    inv = jnp.broadcast_to(inv, (rows, HD))
    inverse[...] = inv
    for i in range(width // HD):
        s = slice(i * HD, (i + 1) * HD)
        queries[:, s] = (stream[:, s].astype(jnp.float32) * inv * gain[:, s]).astype(jnp.bfloat16)


def prepare(info, stream, gain, own, near, far, partners):
    rows, width = stream.shape
    kvw = own.shape[1] // 2
    groups = kvw // HD
    return pl.pallas_call(
        functools.partial(prepare_kernel, len(partners)),
        out_shape=[
            jax.ShapeDtypeStruct((rows, width), jnp.bfloat16),
            jax.ShapeDtypeStruct((rows, HD), jnp.float32),
            jax.ShapeDtypeStruct((4 * rows, 2 * kvw), jnp.bfloat16),
            jax.ShapeDtypeStruct((groups, HD, 4 * rows), jnp.bfloat16),
        ],
        in_specs=[SMEM] + [VMEM] * (5 + len(partners)),
        out_specs=[VMEM] * 4,
        compiler_params=params(VM_SMALL),
        cost_estimate=cost(6.0),
    )(info, stream, gain, own, near, far, *partners)


def local_kernel(info, cot, queries, slots, raised_all, gws_all, peaks, totals, weighted):
    rows, width = cot.shape
    kvw = slots.shape[1] // 2
    count = raised_all.shape[0]
    pairs = count // (kvw // HD)
    scale = HD**-0.5 * math.log2(math.e)
    me, devices = info[0], info[1]
    valid = (me > 0, None, me < devices - 1, None)

    def stack(ref, i):
        at = 2 * i * HD
        return jnp.concatenate([ref[:, at : at + HD], ref[:, at + HD : at + 2 * HD]], axis=0)

    for i in range(count):
        g = i // pairs
        scores = dot(slots[:, g * HD : (g + 1) * HD], stack(queries, i), NT)
        gws = dot(slots[:, kvw + g * HD : kvw + (g + 1) * HD], stack(cot, i), NT)
        gws_all[i] = gws
        peak = None
        for j in range(4):
            top = jnp.max(scores[j * rows : (j + 1) * rows], axis=0, keepdims=True)
            if valid[j] is not None:
                top = jnp.where(valid[j], top, -BIG)
            peak = top if peak is None else jnp.maximum(peak, top)
        peak = peak * scale
        total = 0.0
        product = 0.0
        for j in range(4):
            s = slice(j * rows, (j + 1) * rows)
            shift = peak if valid[j] is None else jnp.where(valid[j], peak, BIG)
            e = jnp.exp2(scores[s] * scale - shift)
            total = total + jnp.sum(e, axis=0, keepdims=True)
            product = product + jnp.sum(e * gws[s], axis=0, keepdims=True)
            raised_all[i, s] = e
        peaks[i] = peak
        totals[i] = total
        weighted[i] = product


def local(info, cot, queries, slots):
    rows, width = cot.shape
    count = width // HD // 2
    tall = jax.ShapeDtypeStruct((count, 4 * rows, 2 * rows), jnp.float32)
    flat = jax.ShapeDtypeStruct((count, 1, 2 * rows), jnp.float32)
    return pl.pallas_call(
        local_kernel,
        out_shape=[tall, tall, flat, flat, flat],
        in_specs=[SMEM] + [VMEM] * 3,
        out_specs=[VMEM] * 5,
        compiler_params=params(VM_LOCAL),
        cost_estimate=cost(6.0),
    )(info, cot, queries, slots)


def attend_kernel(info, stream, cot, gain, queries, inverse, key_cols, raised_all, gws_all, peaks, totals,
                  weighted_all, even_block, odd_block, handed, keep_g, beside_g, across_g, corner_g,
                  low_all, grad_all, dq, products, dk, dv, block, block_t, w0, d0, w1, d1):
    rows, width = stream.shape
    groups = key_cols.shape[0]
    kvw = groups * HD
    heads = width // HD
    pairs = heads // groups // 2
    count = groups * pairs
    factor = HD**-0.5
    scale = factor * math.log2(math.e)
    me = info[0]
    valid = me > 0
    block[...] = jnp.where(me % 2 == 1, odd_block[...], even_block[...])
    for g in range(groups):
        block_t[g] = block[:, g * HD : (g + 1) * HD].T

    def stack(ref, i):
        at = 2 * i * HD
        return jnp.concatenate([ref[:, at : at + HD], ref[:, at + HD : at + 2 * HD]], axis=0)

    def columns(i):
        return slice((i % pairs) * 2 * rows, (i % pairs + 1) * 2 * rows)

    def weigh(i, low, grad):
        g = i // pairs
        kc = slice(g * HD, (g + 1) * HD)
        vc = slice(kvw + g * HD, kvw + (g + 1) * HD)
        s1, g1 = dot(block[:, kc], stack(queries, i), NT), dot(block[:, vc], stack(cot, i), NT)
        top = jnp.where(valid, jnp.max(s1, axis=0, keepdims=True) * scale, -BIG)
        peak = jnp.maximum(peaks[i], top)
        fade = jnp.exp2(peaks[i] - peak)
        e = jnp.exp2(s1 * scale - jnp.where(valid, peak, BIG))
        total = totals[i] * fade + jnp.sum(e, axis=0, keepdims=True)
        weighted = weighted_all[i] * fade + jnp.sum(e * g1, axis=0, keepdims=True)
        share = 1.0 / total
        centre = weighted * share
        fade = fade * share
        for j in range(4):
            at = slice(j * rows, (j + 1) * rows)
            w = raised_all[i, at] * fade
            low_all[g, at, columns(i)] = w.astype(jnp.bfloat16)
            grad_all[g, at, columns(i)] = (w * (gws_all[i, at] - centre)).astype(jnp.bfloat16)
        w = e * share
        low[...] = w.astype(jnp.bfloat16)
        grad[...] = (w * (g1 - centre)).astype(jnp.bfloat16)

    def spread(i, low, grad):
        g = i // pairs
        value_part = dot(low[...], stack(cot, i), NN)
        key_part = dot(grad[...], stack(queries, i), NN)
        if i % pairs == 0:
            dv[g] = value_part
            dk[g] = key_part
        else:
            dv[g] += value_part
            dk[g] += key_part
        cols = dot(key_cols[g], grad_all[g, :, columns(i)], NN) + dot(block_t[g], grad[...], NN)
        back = cols.T
        for h in range(2):
            s = slice((2 * i + h) * HD, (2 * i + h + 1) * HD)
            part = back[h * rows : (h + 1) * rows] * (gain[:, s] * factor)
            dq[:, s] = part
            products[...] += part * stream[:, s].astype(jnp.float32)

    products[...] = jnp.zeros_like(products)
    buffers = ((w0, d0), (w1, d1))
    weigh(0, *buffers[0])
    for i in range(1, count):
        weigh(i, *buffers[i % 2])
        spread(i - 1, *buffers[(i - 1) % 2])
    spread(count - 1, *buffers[(count - 1) % 2])

    inv = inverse[...]
    mean = jnp.sum(products[...], axis=1, keepdims=True) * (1.0 / width) * inv
    pull = inv * inv * mean
    for i in range(width // HD):
        s = slice(i * HD, (i + 1) * HD)
        x = stream[:, s].astype(jnp.float32)
        grad_hidden = dq[:, s] * inv - x * pull
        handed[:, s] = (cot[:, s].astype(jnp.float32) + grad_hidden).astype(jnp.bfloat16)

    share = rows // 4

    def share_at(mask):
        return pl.ds(pl.multiple_of(((me % 4) ^ mask) * share, share), share)

    for g in range(groups):
        kc = slice(g * HD, (g + 1) * HD)
        vc = slice(kvw + g * HD, kvw + (g + 1) * HD)
        dk[g] = dk[g] * factor
        for source, cols in ((dk, kc), (dv, vc)):
            keep_g[:, cols] = source[g, share_at(0)]
            beside_g[:, cols] = source[g, share_at(1)].astype(jnp.bfloat16)
            across_g[:, cols] = source[g, share_at(2)].astype(jnp.bfloat16)
            corner_g[:, cols] = source[g, share_at(3)].astype(jnp.bfloat16)


def attend(info, stream, cot, gain, queries, inverse, key_cols, locals_, even_block, odd_block):
    rows, width = stream.shape
    groups = key_cols.shape[0]
    kvw = groups * HD
    kept = jax.ShapeDtypeStruct((rows // 4, 2 * kvw), jnp.float32)
    share = jax.ShapeDtypeStruct((rows // 4, 2 * kvw), jnp.bfloat16)
    tall = jax.ShapeDtypeStruct((groups, 4 * rows, rows * width // (HD * groups)), jnp.bfloat16)
    return pl.pallas_call(
        attend_kernel,
        out_shape=[jax.ShapeDtypeStruct((rows, width), jnp.bfloat16), kept, share, share, share, tall, tall],
        in_specs=[SMEM] + [VMEM] * 13,
        out_specs=[VMEM] * 7,
        scratch_shapes=[
            pltpu.VMEM((rows, width), jnp.float32),
            pltpu.VMEM((rows, HD), jnp.float32),
            pltpu.VMEM((groups, rows, HD), jnp.float32),
            pltpu.VMEM((groups, rows, HD), jnp.float32),
            pltpu.VMEM((rows, 2 * kvw), jnp.bfloat16),
            pltpu.VMEM((groups, HD, rows), jnp.bfloat16),
        ]
        + [pltpu.VMEM((rows, 2 * rows), jnp.bfloat16)] * 4,
        compiler_params=params(VM_ATTEND),
        cost_estimate=cost(12.0),
    )(info, stream, cot, gain, queries, inverse, key_cols, *locals_, even_block, odd_block)


def terms_kernel(partner_count, info, cot, queries, low_all, grad_all, *outs):
    own_g, near_g, far_g = outs[:3]
    partners_g = outs[3 : 3 + partner_count]
    term = outs[3 + partner_count]
    rows, width = cot.shape
    groups = low_all.shape[0]
    kvw = groups * HD
    each = width // groups // HD
    factor = HD**-0.5
    me, want = info[0], info[2]
    odd = me % 2
    near_at = pl.multiple_of((1 - odd) * 2 * rows, rows)
    far_at = pl.multiple_of(odd * 2 * rows, rows)
    for g in range(groups):
        for part, (weights, ref, base) in enumerate(((grad_all, queries, 0), (low_all, cot, kvw))):
            heads = [ref[:, (g * each + h) * HD : (g * each + h + 1) * HD] for h in range(each)]
            n = 2 * g + part
            cols = slice(base + g * HD, base + (g + 1) * HD)
            sums = dot(weights[g], jnp.concatenate(heads, axis=0), NN)
            term[n] = sums * factor if part == 0 else sums
            own_g[:, cols] = term[n, rows : 2 * rows]
            near_g[:, cols] = term[n, pl.ds(near_at, rows)].astype(jnp.bfloat16)
            far_g[:, cols] = term[n, pl.ds(far_at, rows)].astype(jnp.bfloat16)
            picked = term[n, 3 * rows : 4 * rows].astype(jnp.bfloat16)
            for b in range(partner_count):
                hit = want == (me ^ (2 << b))
                partners_g[b][:, cols] = jnp.where(hit, picked, jnp.zeros_like(picked))


def terms_of(info, cot, queries, low_all, grad_all, partner_count):
    rows = cot.shape[0]
    groups = low_all.shape[0]
    kvw = groups * HD
    low = jax.ShapeDtypeStruct((rows, 2 * kvw), jnp.bfloat16)
    wide = jax.ShapeDtypeStruct((rows, 2 * kvw), jnp.float32)
    return pl.pallas_call(
        functools.partial(terms_kernel, partner_count),
        out_shape=[wide, low, low] + [low] * partner_count,
        in_specs=[SMEM] + [VMEM] * 4,
        out_specs=[VMEM] * (3 + partner_count),
        scratch_shapes=[pltpu.VMEM((2 * groups, 4 * rows, HD), jnp.float32)],
        compiler_params=params(VM_TERMS),
        cost_estimate=cost(5.0),
    )(info, cot, queries, low_all, grad_all)


def collect_kernel(own, *rest):
    total = own[...]
    for ref in rest[:-1]:
        total = total + ref[...].astype(jnp.float32)
    rest[-1][...] = total


def collect(own, parts):
    return pl.pallas_call(
        collect_kernel,
        out_shape=jax.ShapeDtypeStruct(own.shape, jnp.float32),
        in_specs=[VMEM] * (1 + len(parts)),
        out_specs=VMEM,
        compiler_params=params(VM_SMALL),
        cost_estimate=cost(0.5),
    )(own, *parts)


def finish_kernel(part_count, info, received, own, acc, *rest):
    previous, keys, values = rest[-3:]
    parts = rest[:part_count]
    terms = rest[part_count:-6]
    others = rest[-6:-3]
    previous[...] = received[...]
    kvw = keys.shape[1]
    rows = acc.shape[0]
    first = info[0] == 0
    last = acc[...]
    for ref in terms:
        last = last + ref[...].astype(jnp.float32)
    for k in range(4):
        at = slice(k * rows, (k + 1) * rows)
        total = own[at, :]
        for ref in parts:
            total = total + ref[at, :].astype(jnp.float32)
        part = last if k == 0 else others[k - 1][...].astype(jnp.float32)
        result = (total + jnp.where(first, part, 0.0)).astype(jnp.bfloat16)
        keys[at, :] = result[:, :kvw]
        values[at, :] = result[:, kvw:]


def finish(info, received, own, parts, acc, terms, others):
    shape = jax.ShapeDtypeStruct((own.shape[0], own.shape[1] // 2), jnp.bfloat16)
    return pl.pallas_call(
        functools.partial(finish_kernel, len(parts)),
        out_shape=[jax.ShapeDtypeStruct(received.shape, received.dtype), shape, shape],
        in_specs=[SMEM] + [VMEM] * (3 + len(parts) + len(terms) + len(others)),
        out_specs=[VMEM] * 3,
        compiler_params=params(VM_SMALL),
        cost_estimate=cost(0.5),
    )(info, received, own, acc, *parts, *terms, *others)


def permuted(value, pairs, axis="seq"):
    return lax.ppermute(value, axis, pairs)


def global_rounds(count, have):
    missing = [i for i in range(0, count, 2) if i not in have]
    rounds = []
    while missing:
        pairs = []
        for source in sorted(have, reverse=True):
            free = [t for t in missing if t not in [p[1] for p in pairs]]
            if free:
                best = min(free, key=lambda t: (bin(t ^ source).count("1"), abs(t - source)))
                pairs.append((source, best))
        rounds.append(pairs)
        have = have + [t for _, t in pairs]
        missing = [i for i in missing if i not in have]
    return rounds


def among(device, members):
    hit = device == members[0]
    for member in members[1:]:
        hit = hit | (device == member)
    return hit


def on_device(stream, cotangent, keys, values, gain, rand_blocks):
    hidden = stream[0]
    upstream = cotangent[0]
    count = lax.axis_size("seq")
    bits = count.bit_length() - 1
    device = lax.axis_index("seq")
    own = jnp.concatenate([keys[0], values[0]], axis=1)
    swaps = [[(i, i ^ (1 << b)) for i in range(count)] for b in range(bits)]
    across = [(i, i + 1) for i in range(1, count - 1, 2)]
    across = across + [(j, i) for i, j in across]
    info = jnp.stack([device, jnp.int32(count), rand_blocks[0, 0]])

    top = count // 4 * 3
    partners = [None] * bits
    for b in reversed(range(2, bits)):
        partners[b] = permuted(own, swaps[b])
    block_top = permuted(own, [(0, top)])
    partners[1] = permuted(own, swaps[1])
    far = permuted(own, across)
    near = permuted(own, swaps[0])

    block0 = jnp.where(device == top, block_top, own)
    for b in range(1, bits):
        block0 = jnp.where(device == (1 << b), partners[b], block0)
    block0, far = lax.optimization_barrier((block0, far))
    for pairs in global_rounds(count, [0, top] + [1 << b for b in range(1, bits)]):
        masks = {i ^ j for i, j in pairs}
        if len(masks) == 1:
            route = swaps[masks.pop().bit_length() - 1]
        else:
            route = pairs
        moved = permuted(block0, route)
        block0 = jnp.where(among(device, [t for _, t in pairs]), moved, block0)
    queries, inverse, slots, key_cols = prepare(info, hidden, gain, own, near, far, partners[1:])
    locals_ = list(local(info, upstream, queries, slots))
    block0, locals_[2] = lax.optimization_barrier((block0, locals_[2]))
    odd_block = permuted(block0, swaps[0])
    handed, keep_g, beside_g, across_g, corner_g, low_all, grad_all = attend(
        info, hidden, upstream, gain, queries, inverse, key_cols, locals_, block0, odd_block
    )
    outs = terms_of(info, upstream, queries, low_all, grad_all, bits - 1)
    own_g, near_g, far_g = outs[:3]
    partners_g = outs[3:]

    sections = lax.axis_size("section")
    back = [((i + 1) % sections, i) for i in range(sections)]
    rows = own.shape[0]

    def swapped(value, mask):
        return permuted(value, [(i, i ^ mask) for i in range(count)])

    received = permuted(handed, back, "section")
    near_r = permuted(near_g, swaps[0])
    y_r = permuted(partners_g[0], swaps[1])
    far_r = permuted(far_g, across)
    z_r = [permuted(partners_g[b - 1], swaps[b]) for b in range(2, bits)]

    terms = [swapped(beside_g, 1), swapped(across_g, 2), swapped(corner_g, 3)]
    acc = keep_g
    for b in range(2, bits, 2):
        acc = acc + sum(t.astype(jnp.float32) for t in terms)
        low = acc.astype(jnp.bfloat16)
        terms = [swapped(low, k << b) for k in range(1, 1 << min(2, bits - b))]
    mine = (acc + sum(t.astype(jnp.float32) for t in terms)).astype(jnp.bfloat16)
    others = [swapped(mine, mask) for mask in (1, 2, 3)]
    own_g = collect(own_g, z_r)
    parts = [near_r, y_r, far_r]
    previous, key_grads, value_grads = finish(info, received, own_g, parts, acc, terms, others)
    return (previous[None], key_grads[None], value_grads[None])


def solution(mesh):
    return jax.shard_map(
        on_device,
        mesh=mesh,
        in_specs=(
            P("section", "seq", None),
            P("section", "seq", None),
            P("section", "seq", None),
            P("section", "seq", None),
            P("section", None),
            P("seq", None),
        ),
        out_specs=(P("section", "seq", None), P("section", "seq", None), P("section", "seq", None)),
        check_vma=False,
    )
```

```python
import functools
import math

import jax
import jax.numpy as jnp
from jax import lax
from jax.experimental import pallas as pl
from jax.experimental.pallas import tpu as pltpu
from jax.sharding import PartitionSpec as P

HD = 128
BIG = 1e30
MEGA = 1 << 20
VM_SMALL = 6
VM_LOCAL = 6
VM_TERMS = 6
VM_ATTEND = 8

NT = (((1,), (1,)), ((), ()))
NN = (((1,), (0,)), ((), ()))


def dot(a, b, dims):
    return lax.dot_general(a, b, dims, preferred_element_type=jnp.float32)


def cost(micros):
    return pl.CostEstimate(flops=int(micros * 1.15e9), bytes_accessed=MEGA, transcendentals=0)


def params(megas):
    return pltpu.CompilerParams(vmem_limit_bytes=megas * MEGA)


VMEM = pl.BlockSpec(memory_space=pltpu.VMEM)
SMEM = pl.BlockSpec(memory_space=pltpu.SMEM)


def norm_kernel(stream, gain, queries, inverse):
    rows, width = stream.shape
    squares = jnp.zeros((rows, HD), jnp.float32)
    for i in range(width // HD):
        x = stream[:, i * HD : (i + 1) * HD].astype(jnp.float32)
        squares = squares + x * x
    inv = lax.rsqrt(jnp.sum(squares, axis=1, keepdims=True) / width + 1e-5)
    inv = jnp.broadcast_to(inv, (rows, HD))
    inverse[...] = inv
    for i in range(width // HD):
        s = slice(i * HD, (i + 1) * HD)
        queries[:, s] = (stream[:, s].astype(jnp.float32) * inv * gain[:, s]).astype(jnp.bfloat16)


def norm(stream, gain):
    rows, width = stream.shape
    return pl.pallas_call(
        norm_kernel,
        out_shape=[jax.ShapeDtypeStruct((rows, width), jnp.bfloat16), jax.ShapeDtypeStruct((rows, HD), jnp.float32)],
        in_specs=[VMEM] * 2,
        out_specs=[VMEM] * 2,
        compiler_params=params(VM_SMALL),
        cost_estimate=cost(2.0),
    )(stream, gain)


def arrange_kernel(partner_count, info, own, near, far, *rest):
    partners = rest[:partner_count]
    slots, key_cols = rest[partner_count:]
    rows = own.shape[0]
    me, want = info[0], info[2]
    odd = me % 2
    near_at = pl.multiple_of((1 - odd) * 2 * rows, rows)
    far_at = pl.multiple_of(odd * 2 * rows, rows)
    slots[rows : 2 * rows, :] = own[...]
    slots[pl.ds(near_at, rows), :] = near[...]
    slots[pl.ds(far_at, rows), :] = far[...]
    slots[3 * rows : 4 * rows, :] = partners[0][...]
    for b in range(1, partner_count):
        @pl.when(want == (me ^ (2 << b)))
        def _():
            slots[3 * rows : 4 * rows, :] = partners[b][...]
    for g in range(key_cols.shape[0]):
        key_cols[g] = slots[:, g * HD : (g + 1) * HD].T


def arrange(info, own, near, far, partners):
    rows = own.shape[0]
    kvw = own.shape[1] // 2
    return pl.pallas_call(
        functools.partial(arrange_kernel, len(partners)),
        out_shape=[
            jax.ShapeDtypeStruct((4 * rows, 2 * kvw), jnp.bfloat16),
            jax.ShapeDtypeStruct((kvw // HD, HD, 4 * rows), jnp.bfloat16),
        ],
        in_specs=[SMEM] + [VMEM] * (3 + len(partners)),
        out_specs=[VMEM] * 2,
        compiler_params=params(VM_SMALL),
        cost_estimate=cost(1.0),
    )(info, own, near, far, *partners)


def local_kernel(info, cot, queries, slots, raised_all, gws_all, peaks, totals, weighted):
    rows, width = cot.shape
    kvw = slots.shape[1] // 2
    count = raised_all.shape[0]
    pairs = count // (kvw // HD)
    scale = HD**-0.5 * math.log2(math.e)
    me, devices = info[0], info[1]
    valid = (me > 0, None, me < devices - 1, None)

    def stack(ref, i):
        at = 2 * i * HD
        return jnp.concatenate([ref[:, at : at + HD], ref[:, at + HD : at + 2 * HD]], axis=0)

    for i in range(count):
        g = i // pairs
        scores = dot(slots[:, g * HD : (g + 1) * HD], stack(queries, i), NT)
        gws = dot(slots[:, kvw + g * HD : kvw + (g + 1) * HD], stack(cot, i), NT)
        gws_all[i] = gws
        peak = None
        for j in range(4):
            top = jnp.max(scores[j * rows : (j + 1) * rows], axis=0, keepdims=True)
            if valid[j] is not None:
                top = jnp.where(valid[j], top, -BIG)
            peak = top if peak is None else jnp.maximum(peak, top)
        peak = peak * scale
        total = 0.0
        product = 0.0
        for j in range(4):
            s = slice(j * rows, (j + 1) * rows)
            shift = peak if valid[j] is None else jnp.where(valid[j], peak, BIG)
            e = jnp.exp2(scores[s] * scale - shift)
            total = total + jnp.sum(e, axis=0, keepdims=True)
            product = product + jnp.sum(e * gws[s], axis=0, keepdims=True)
            raised_all[i, s] = e
        peaks[i] = peak
        totals[i] = total
        weighted[i] = product


def local(info, cot, queries, slots):
    rows, width = cot.shape
    count = width // HD // 2
    tall = jax.ShapeDtypeStruct((count, 4 * rows, 2 * rows), jnp.float32)
    flat = jax.ShapeDtypeStruct((count, 1, 2 * rows), jnp.float32)
    return pl.pallas_call(
        local_kernel,
        out_shape=[tall, tall, flat, flat, flat],
        in_specs=[SMEM] + [VMEM] * 3,
        out_specs=[VMEM] * 5,
        compiler_params=params(VM_LOCAL),
        cost_estimate=cost(6.0),
    )(info, cot, queries, slots)


def attend_kernel(info, stream, cot, gain, queries, inverse, key_cols, raised_all, gws_all, peaks, totals,
                  weighted_all, even_block, odd_block, handed, keep_g, beside_g, across_g, corner_g,
                  low_all, grad_all, dq, products, dk, dv, block, block_t, w0, d0, w1, d1):
    rows, width = stream.shape
    groups = key_cols.shape[0]
    kvw = groups * HD
    heads = width // HD
    pairs = heads // groups // 2
    count = groups * pairs
    factor = HD**-0.5
    scale = factor * math.log2(math.e)
    me = info[0]
    valid = me > 0
    block[...] = jnp.where(me % 2 == 1, odd_block[...], even_block[...])
    for g in range(groups):
        block_t[g] = block[:, g * HD : (g + 1) * HD].T

    def stack(ref, i):
        at = 2 * i * HD
        return jnp.concatenate([ref[:, at : at + HD], ref[:, at + HD : at + 2 * HD]], axis=0)

    def columns(i):
        return slice((i % pairs) * 2 * rows, (i % pairs + 1) * 2 * rows)

    def weigh(i, low, grad):
        g = i // pairs
        kc = slice(g * HD, (g + 1) * HD)
        vc = slice(kvw + g * HD, kvw + (g + 1) * HD)
        s1, g1 = dot(block[:, kc], stack(queries, i), NT), dot(block[:, vc], stack(cot, i), NT)
        top = jnp.where(valid, jnp.max(s1, axis=0, keepdims=True) * scale, -BIG)
        peak = jnp.maximum(peaks[i], top)
        fade = jnp.exp2(peaks[i] - peak)
        e = jnp.exp2(s1 * scale - jnp.where(valid, peak, BIG))
        total = totals[i] * fade + jnp.sum(e, axis=0, keepdims=True)
        weighted = weighted_all[i] * fade + jnp.sum(e * g1, axis=0, keepdims=True)
        share = 1.0 / total
        centre = weighted * share
        fade = fade * share
        for j in range(4):
            at = slice(j * rows, (j + 1) * rows)
            w = raised_all[i, at] * fade
            low_all[g, at, columns(i)] = w.astype(jnp.bfloat16)
            grad_all[g, at, columns(i)] = (w * (gws_all[i, at] - centre)).astype(jnp.bfloat16)
        w = e * share
        low[...] = w.astype(jnp.bfloat16)
        grad[...] = (w * (g1 - centre)).astype(jnp.bfloat16)

    def spread(i, low, grad):
        g = i // pairs
        value_part = dot(low[...], stack(cot, i), NN)
        key_part = dot(grad[...], stack(queries, i), NN)
        if i % pairs == 0:
            dv[g] = value_part
            dk[g] = key_part
        else:
            dv[g] += value_part
            dk[g] += key_part
        cols = dot(key_cols[g], grad_all[g, :, columns(i)], NN) + dot(block_t[g], grad[...], NN)
        back = cols.T
        for h in range(2):
            s = slice((2 * i + h) * HD, (2 * i + h + 1) * HD)
            part = back[h * rows : (h + 1) * rows] * (gain[:, s] * factor)
            dq[:, s] = part
            products[...] += part * stream[:, s].astype(jnp.float32)

    products[...] = jnp.zeros_like(products)
    buffers = ((w0, d0), (w1, d1))
    weigh(0, *buffers[0])
    for i in range(1, count):
        weigh(i, *buffers[i % 2])
        spread(i - 1, *buffers[(i - 1) % 2])
    spread(count - 1, *buffers[(count - 1) % 2])

    inv = inverse[...]
    mean = jnp.sum(products[...], axis=1, keepdims=True) * (1.0 / width) * inv
    pull = inv * inv * mean
    for i in range(width // HD):
        s = slice(i * HD, (i + 1) * HD)
        x = stream[:, s].astype(jnp.float32)
        grad_hidden = dq[:, s] * inv - x * pull
        handed[:, s] = (cot[:, s].astype(jnp.float32) + grad_hidden).astype(jnp.bfloat16)

    share = rows // 4

    def share_at(mask):
        return pl.ds(pl.multiple_of(((me % 4) ^ mask) * share, share), share)

    for g in range(groups):
        kc = slice(g * HD, (g + 1) * HD)
        vc = slice(kvw + g * HD, kvw + (g + 1) * HD)
        dk[g] = dk[g] * factor
        for source, cols in ((dk, kc), (dv, vc)):
            keep_g[:, cols] = source[g, share_at(0)]
            beside_g[:, cols] = source[g, share_at(1)].astype(jnp.bfloat16)
            across_g[:, cols] = source[g, share_at(2)].astype(jnp.bfloat16)
            corner_g[:, cols] = source[g, share_at(3)].astype(jnp.bfloat16)


def attend(info, stream, cot, gain, queries, inverse, key_cols, locals_, even_block, odd_block):
    rows, width = stream.shape
    groups = key_cols.shape[0]
    kvw = groups * HD
    kept = jax.ShapeDtypeStruct((rows // 4, 2 * kvw), jnp.float32)
    share = jax.ShapeDtypeStruct((rows // 4, 2 * kvw), jnp.bfloat16)
    tall = jax.ShapeDtypeStruct((groups, 4 * rows, rows * width // (HD * groups)), jnp.bfloat16)
    return pl.pallas_call(
        attend_kernel,
        out_shape=[jax.ShapeDtypeStruct((rows, width), jnp.bfloat16), kept, share, share, share, tall, tall],
        in_specs=[SMEM] + [VMEM] * 13,
        out_specs=[VMEM] * 7,
        scratch_shapes=[
            pltpu.VMEM((rows, width), jnp.float32),
            pltpu.VMEM((rows, HD), jnp.float32),
            pltpu.VMEM((groups, rows, HD), jnp.float32),
            pltpu.VMEM((groups, rows, HD), jnp.float32),
            pltpu.VMEM((rows, 2 * kvw), jnp.bfloat16),
            pltpu.VMEM((groups, HD, rows), jnp.bfloat16),
        ]
        + [pltpu.VMEM((rows, 2 * rows), jnp.bfloat16)] * 4,
        compiler_params=params(VM_ATTEND),
        cost_estimate=cost(12.0),
    )(info, stream, cot, gain, queries, inverse, key_cols, *locals_, even_block, odd_block)


def terms_kernel(partner_count, info, cot, queries, low_all, grad_all, *outs):
    own_g, near_g, far_g = outs[:3]
    partners_g = outs[3 : 3 + partner_count]
    term = outs[3 + partner_count]
    rows, width = cot.shape
    groups = low_all.shape[0]
    kvw = groups * HD
    each = width // groups // HD
    factor = HD**-0.5
    me, want = info[0], info[2]
    odd = me % 2
    near_at = pl.multiple_of((1 - odd) * 2 * rows, rows)
    far_at = pl.multiple_of(odd * 2 * rows, rows)
    for g in range(groups):
        for part, (weights, ref, base) in enumerate(((grad_all, queries, 0), (low_all, cot, kvw))):
            heads = [ref[:, (g * each + h) * HD : (g * each + h + 1) * HD] for h in range(each)]
            n = 2 * g + part
            cols = slice(base + g * HD, base + (g + 1) * HD)
            sums = dot(weights[g], jnp.concatenate(heads, axis=0), NN)
            term[n] = sums * factor if part == 0 else sums
            own_g[:, cols] = term[n, rows : 2 * rows]
            near_g[:, cols] = term[n, pl.ds(near_at, rows)].astype(jnp.bfloat16)
            far_g[:, cols] = term[n, pl.ds(far_at, rows)].astype(jnp.bfloat16)
            picked = term[n, 3 * rows : 4 * rows].astype(jnp.bfloat16)
            for b in range(partner_count):
                hit = want == (me ^ (2 << b))
                partners_g[b][:, cols] = jnp.where(hit, picked, jnp.zeros_like(picked))


def terms_of(info, cot, queries, low_all, grad_all, partner_count):
    rows = cot.shape[0]
    groups = low_all.shape[0]
    kvw = groups * HD
    low = jax.ShapeDtypeStruct((rows, 2 * kvw), jnp.bfloat16)
    wide = jax.ShapeDtypeStruct((rows, 2 * kvw), jnp.float32)
    return pl.pallas_call(
        functools.partial(terms_kernel, partner_count),
        out_shape=[wide, low, low] + [low] * partner_count,
        in_specs=[SMEM] + [VMEM] * 4,
        out_specs=[VMEM] * (3 + partner_count),
        scratch_shapes=[pltpu.VMEM((2 * groups, 4 * rows, HD), jnp.float32)],
        compiler_params=params(VM_TERMS),
        cost_estimate=cost(5.0),
    )(info, cot, queries, low_all, grad_all)


def collect_kernel(own, *rest):
    total = own[...]
    for ref in rest[:-1]:
        total = total + ref[...].astype(jnp.float32)
    rest[-1][...] = total


def collect(own, parts):
    return pl.pallas_call(
        collect_kernel,
        out_shape=jax.ShapeDtypeStruct(own.shape, jnp.float32),
        in_specs=[VMEM] * (1 + len(parts)),
        out_specs=VMEM,
        compiler_params=params(VM_SMALL),
        cost_estimate=cost(0.5),
    )(own, *parts)


def finish_kernel(part_count, info, received, own, acc, *rest):
    previous, keys, values = rest[-3:]
    parts = rest[:part_count]
    terms = rest[part_count:-6]
    others = rest[-6:-3]
    previous[...] = received[...]
    kvw = keys.shape[1]
    rows = acc.shape[0]
    first = info[0] == 0
    last = acc[...]
    for ref in terms:
        last = last + ref[...].astype(jnp.float32)
    for k in range(4):
        at = slice(k * rows, (k + 1) * rows)
        total = own[at, :]
        for ref in parts:
            total = total + ref[at, :].astype(jnp.float32)
        part = last if k == 0 else others[k - 1][...].astype(jnp.float32)
        result = (total + jnp.where(first, part, 0.0)).astype(jnp.bfloat16)
        keys[at, :] = result[:, :kvw]
        values[at, :] = result[:, kvw:]


def finish(info, received, own, parts, acc, terms, others):
    shape = jax.ShapeDtypeStruct((own.shape[0], own.shape[1] // 2), jnp.bfloat16)
    return pl.pallas_call(
        functools.partial(finish_kernel, len(parts)),
        out_shape=[jax.ShapeDtypeStruct(received.shape, received.dtype), shape, shape],
        in_specs=[SMEM] + [VMEM] * (3 + len(parts) + len(terms) + len(others)),
        out_specs=[VMEM] * 3,
        compiler_params=params(VM_SMALL),
        cost_estimate=cost(0.5),
    )(info, received, own, acc, *parts, *terms, *others)


def permuted(value, pairs, axis="seq"):
    return lax.ppermute(value, axis, pairs)


def global_rounds(count, have):
    missing = [i for i in range(0, count, 2) if i not in have]
    rounds = []
    while missing:
        pairs = []
        for source in sorted(have, reverse=True):
            free = [t for t in missing if t not in [p[1] for p in pairs]]
            if free:
                best = min(free, key=lambda t: (bin(t ^ source).count("1"), abs(t - source)))
                pairs.append((source, best))
        rounds.append(pairs)
        have = have + [t for _, t in pairs]
        missing = [i for i in missing if i not in have]
    return rounds


def among(device, members):
    hit = device == members[0]
    for member in members[1:]:
        hit = hit | (device == member)
    return hit


def on_device(stream, cotangent, keys, values, gain, rand_blocks):
    hidden = stream[0]
    upstream = cotangent[0]
    count = lax.axis_size("seq")
    bits = count.bit_length() - 1
    device = lax.axis_index("seq")
    own = jnp.concatenate([keys[0], values[0]], axis=1)
    swaps = [[(i, i ^ (1 << b)) for i in range(count)] for b in range(bits)]
    across = [(i, i + 1) for i in range(1, count - 1, 2)]
    across = across + [(j, i) for i, j in across]
    info = jnp.stack([device, jnp.int32(count), rand_blocks[0, 0]])

    top = count // 4 * 3
    partners = [None] * bits
    for b in reversed(range(2, bits)):
        partners[b] = permuted(own, swaps[b])
    block_top = permuted(own, [(0, top)])
    partners[1] = permuted(own, swaps[1])
    far = permuted(own, across)
    near = permuted(own, swaps[0])

    block0 = jnp.where(device == top, block_top, own)
    for b in range(1, bits):
        block0 = jnp.where(device == (1 << b), partners[b], block0)
    kept, near = lax.optimization_barrier((gain, near))
    queries, inverse = norm(hidden, kept)
    block0, far, inverse = lax.optimization_barrier((block0, far, inverse))
    for pairs in global_rounds(count, [0, top] + [1 << b for b in range(1, bits)]):
        masks = {i ^ j for i, j in pairs}
        if len(masks) == 1:
            route = swaps[masks.pop().bit_length() - 1]
        else:
            route = pairs
        moved = permuted(block0, route)
        block0 = jnp.where(among(device, [t for _, t in pairs]), moved, block0)
    slots, key_cols = arrange(info, own, near, far, partners[1:])
    locals_ = list(local(info, upstream, queries, slots))
    block0, locals_[2] = lax.optimization_barrier((block0, locals_[2]))
    odd_block = permuted(block0, swaps[0])
    handed, keep_g, beside_g, across_g, corner_g, low_all, grad_all = attend(
        info, hidden, upstream, gain, queries, inverse, key_cols, locals_, block0, odd_block
    )
    outs = terms_of(info, upstream, queries, low_all, grad_all, bits - 1)
    own_g, near_g, far_g = outs[:3]
    partners_g = outs[3:]

    sections = lax.axis_size("section")
    back = [((i + 1) % sections, i) for i in range(sections)]
    rows = own.shape[0]

    def swapped(value, mask):
        return permuted(value, [(i, i ^ mask) for i in range(count)])

    received = permuted(handed, back, "section")
    near_r = permuted(near_g, swaps[0])
    y_r = permuted(partners_g[0], swaps[1])
    far_r = permuted(far_g, across)
    z_r = [permuted(partners_g[b - 1], swaps[b]) for b in range(2, bits)]

    terms = [swapped(beside_g, 1), swapped(across_g, 2), swapped(corner_g, 3)]
    acc = keep_g
    for b in range(2, bits, 2):
        acc = acc + sum(t.astype(jnp.float32) for t in terms)
        low = acc.astype(jnp.bfloat16)
        terms = [swapped(low, k << b) for k in range(1, 1 << min(2, bits - b))]
    mine = (acc + sum(t.astype(jnp.float32) for t in terms)).astype(jnp.bfloat16)
    others = [swapped(mine, mask) for mask in (1, 2, 3)]
    own_g = collect(own_g, z_r)
    parts = [near_r, y_r, far_r]
    previous, key_grads, value_grads = finish(info, received, own_g, parts, acc, terms, others)
    return (previous[None], key_grads[None], value_grads[None])


def solution(mesh):
    return jax.shard_map(
        on_device,
        mesh=mesh,
        in_specs=(
            P("section", "seq", None),
            P("section", "seq", None),
            P("section", "seq", None),
            P("section", "seq", None),
            P("section", None),
            P("seq", None),
        ),
        out_specs=(P("section", "seq", None), P("section", "seq", None), P("section", "seq", None)),
        check_vma=False,
    )
```

```python
import functools
import math

import jax
import jax.numpy as jnp
from jax import lax
from jax.experimental import pallas as pl
from jax.experimental.pallas import tpu as pltpu
from jax.sharding import PartitionSpec as P

HD = 128
BIG = 1e30
MEGA = 1 << 20
VM_SMALL = 6
VM_LOCAL = 6
VM_TERMS = 6
VM_ATTEND = 8

NT = (((1,), (1,)), ((), ()))
NN = (((1,), (0,)), ((), ()))


def dot(a, b, dims):
    return lax.dot_general(a, b, dims, preferred_element_type=jnp.float32)


def cost(micros):
    return pl.CostEstimate(flops=int(micros * 1.15e9), bytes_accessed=MEGA, transcendentals=0)


def params(megas):
    return pltpu.CompilerParams(vmem_limit_bytes=megas * MEGA)


VMEM = pl.BlockSpec(memory_space=pltpu.VMEM)
SMEM = pl.BlockSpec(memory_space=pltpu.SMEM)


def norm_kernel(stream, gain, queries, inverse):
    rows, width = stream.shape
    squares = jnp.zeros((rows, HD), jnp.float32)
    for i in range(width // HD):
        x = stream[:, i * HD : (i + 1) * HD].astype(jnp.float32)
        squares = squares + x * x
    inv = lax.rsqrt(jnp.sum(squares, axis=1, keepdims=True) / width + 1e-5)
    inv = jnp.broadcast_to(inv, (rows, HD))
    inverse[...] = inv
    for i in range(width // HD):
        s = slice(i * HD, (i + 1) * HD)
        queries[:, s] = (stream[:, s].astype(jnp.float32) * inv * gain[:, s]).astype(jnp.bfloat16)


def norm(stream, gain):
    rows, width = stream.shape
    return pl.pallas_call(
        norm_kernel,
        out_shape=[jax.ShapeDtypeStruct((rows, width), jnp.bfloat16), jax.ShapeDtypeStruct((rows, HD), jnp.float32)],
        in_specs=[VMEM] * 2,
        out_specs=[VMEM] * 2,
        compiler_params=params(VM_SMALL),
        cost_estimate=cost(2.0),
    )(stream, gain)


def arrange_kernel(partner_count, info, own, near, far, *rest):
    partners = rest[:partner_count]
    slots, key_cols = rest[partner_count:]
    rows = own.shape[0]
    me, want = info[0], info[2]
    odd = me % 2
    near_at = pl.multiple_of((1 - odd) * 2 * rows, rows)
    far_at = pl.multiple_of(odd * 2 * rows, rows)
    slots[rows : 2 * rows, :] = own[...]
    slots[pl.ds(near_at, rows), :] = near[...]
    slots[pl.ds(far_at, rows), :] = far[...]
    slots[3 * rows : 4 * rows, :] = partners[0][...]
    for b in range(1, partner_count):
        @pl.when(want == (me ^ (2 << b)))
        def _():
            slots[3 * rows : 4 * rows, :] = partners[b][...]
    for g in range(key_cols.shape[0]):
        key_cols[g] = slots[:, g * HD : (g + 1) * HD].T


def arrange(info, own, near, far, partners):
    rows = own.shape[0]
    kvw = own.shape[1] // 2
    return pl.pallas_call(
        functools.partial(arrange_kernel, len(partners)),
        out_shape=[
            jax.ShapeDtypeStruct((4 * rows, 2 * kvw), jnp.bfloat16),
            jax.ShapeDtypeStruct((kvw // HD, HD, 4 * rows), jnp.bfloat16),
        ],
        in_specs=[SMEM] + [VMEM] * (3 + len(partners)),
        out_specs=[VMEM] * 2,
        compiler_params=params(VM_SMALL),
        cost_estimate=cost(1.0),
    )(info, own, near, far, *partners)


def local_kernel(info, cot, queries, slots, raised_all, gws_all, peaks, totals, weighted):
    rows, width = cot.shape
    kvw = slots.shape[1] // 2
    count = raised_all.shape[0]
    pairs = count // (kvw // HD)
    scale = HD**-0.5 * math.log2(math.e)
    me, devices = info[0], info[1]
    valid = (me > 0, None, me < devices - 1, None)

    def stack(ref, i):
        at = 2 * i * HD
        return jnp.concatenate([ref[:, at : at + HD], ref[:, at + HD : at + 2 * HD]], axis=0)

    for i in range(count):
        g = i // pairs
        scores = dot(slots[:, g * HD : (g + 1) * HD], stack(queries, i), NT)
        gws = dot(slots[:, kvw + g * HD : kvw + (g + 1) * HD], stack(cot, i), NT)
        gws_all[i] = gws
        peak = None
        for j in range(4):
            top = jnp.max(scores[j * rows : (j + 1) * rows], axis=0, keepdims=True)
            if valid[j] is not None:
                top = jnp.where(valid[j], top, -BIG)
            peak = top if peak is None else jnp.maximum(peak, top)
        peak = peak * scale
        total = 0.0
        product = 0.0
        for j in range(4):
            s = slice(j * rows, (j + 1) * rows)
            shift = peak if valid[j] is None else jnp.where(valid[j], peak, BIG)
            e = jnp.exp2(scores[s] * scale - shift)
            total = total + jnp.sum(e, axis=0, keepdims=True)
            product = product + jnp.sum(e * gws[s], axis=0, keepdims=True)
            raised_all[i, s] = e
        peaks[i] = peak
        totals[i] = total
        weighted[i] = product


def local(info, cot, queries, slots):
    rows, width = cot.shape
    count = width // HD // 2
    tall = jax.ShapeDtypeStruct((count, 4 * rows, 2 * rows), jnp.float32)
    flat = jax.ShapeDtypeStruct((count, 1, 2 * rows), jnp.float32)
    return pl.pallas_call(
        local_kernel,
        out_shape=[tall, tall, flat, flat, flat],
        in_specs=[SMEM] + [VMEM] * 3,
        out_specs=[VMEM] * 5,
        compiler_params=params(VM_LOCAL),
        cost_estimate=cost(6.0),
    )(info, cot, queries, slots)


def attend_kernel(info, stream, cot, gain, queries, inverse, key_cols, raised_all, gws_all, peaks, totals,
                  weighted_all, even_block, odd_block, handed, keep_g, beside_g, across_g, corner_g,
                  low_all, grad_all, dq, products, dk, dv, block, block_t, w0, d0, w1, d1):
    rows, width = stream.shape
    groups = key_cols.shape[0]
    kvw = groups * HD
    heads = width // HD
    pairs = heads // groups // 2
    count = groups * pairs
    factor = HD**-0.5
    scale = factor * math.log2(math.e)
    me = info[0]
    valid = me > 0
    block[...] = jnp.where(me % 2 == 1, odd_block[...], even_block[...])
    for g in range(groups):
        block_t[g] = block[:, g * HD : (g + 1) * HD].T

    def stack(ref, i):
        at = 2 * i * HD
        return jnp.concatenate([ref[:, at : at + HD], ref[:, at + HD : at + 2 * HD]], axis=0)

    def columns(i):
        return slice((i % pairs) * 2 * rows, (i % pairs + 1) * 2 * rows)

    def weigh(i, low, grad):
        g = i // pairs
        kc = slice(g * HD, (g + 1) * HD)
        vc = slice(kvw + g * HD, kvw + (g + 1) * HD)
        s1, g1 = dot(block[:, kc], stack(queries, i), NT), dot(block[:, vc], stack(cot, i), NT)
        top = jnp.where(valid, jnp.max(s1, axis=0, keepdims=True) * scale, -BIG)
        peak = jnp.maximum(peaks[i], top)
        fade = jnp.exp2(peaks[i] - peak)
        e = jnp.exp2(s1 * scale - jnp.where(valid, peak, BIG))
        total = totals[i] * fade + jnp.sum(e, axis=0, keepdims=True)
        weighted = weighted_all[i] * fade + jnp.sum(e * g1, axis=0, keepdims=True)
        share = 1.0 / total
        centre = weighted * share
        fade = fade * share
        for j in range(4):
            at = slice(j * rows, (j + 1) * rows)
            w = raised_all[i, at] * fade
            low_all[g, at, columns(i)] = w.astype(jnp.bfloat16)
            grad_all[g, at, columns(i)] = (w * (gws_all[i, at] - centre)).astype(jnp.bfloat16)
        w = e * share
        low[...] = w.astype(jnp.bfloat16)
        grad[...] = (w * (g1 - centre)).astype(jnp.bfloat16)

    def spread(i, low, grad):
        g = i // pairs
        value_part = dot(low[...], stack(cot, i), NN)
        key_part = dot(grad[...], stack(queries, i), NN)
        if i % pairs == 0:
            dv[g] = value_part
            dk[g] = key_part
        else:
            dv[g] += value_part
            dk[g] += key_part
        cols = dot(key_cols[g], grad_all[g, :, columns(i)], NN) + dot(block_t[g], grad[...], NN)
        back = cols.T
        for h in range(2):
            s = slice((2 * i + h) * HD, (2 * i + h + 1) * HD)
            part = back[h * rows : (h + 1) * rows] * (gain[:, s] * factor)
            dq[:, s] = part
            products[...] += part * stream[:, s].astype(jnp.float32)

    products[...] = jnp.zeros_like(products)
    buffers = ((w0, d0), (w1, d1))
    weigh(0, *buffers[0])
    for i in range(1, count):
        weigh(i, *buffers[i % 2])
        spread(i - 1, *buffers[(i - 1) % 2])
    spread(count - 1, *buffers[(count - 1) % 2])

    inv = inverse[...]
    mean = jnp.sum(products[...], axis=1, keepdims=True) * (1.0 / width) * inv
    pull = inv * inv * mean
    for i in range(width // HD):
        s = slice(i * HD, (i + 1) * HD)
        x = stream[:, s].astype(jnp.float32)
        grad_hidden = dq[:, s] * inv - x * pull
        handed[:, s] = (cot[:, s].astype(jnp.float32) + grad_hidden).astype(jnp.bfloat16)

    share = rows // 4

    def share_at(mask):
        return pl.ds(pl.multiple_of(((me % 4) ^ mask) * share, share), share)

    for g in range(groups):
        kc = slice(g * HD, (g + 1) * HD)
        vc = slice(kvw + g * HD, kvw + (g + 1) * HD)
        dk[g] = dk[g] * factor
        for source, cols in ((dk, kc), (dv, vc)):
            keep_g[:, cols] = source[g, share_at(0)]
            beside_g[:, cols] = source[g, share_at(1)].astype(jnp.bfloat16)
            across_g[:, cols] = source[g, share_at(2)].astype(jnp.bfloat16)
            corner_g[:, cols] = source[g, share_at(3)].astype(jnp.bfloat16)


def attend(info, stream, cot, gain, queries, inverse, key_cols, locals_, even_block, odd_block):
    rows, width = stream.shape
    groups = key_cols.shape[0]
    kvw = groups * HD
    kept = jax.ShapeDtypeStruct((rows // 4, 2 * kvw), jnp.float32)
    share = jax.ShapeDtypeStruct((rows // 4, 2 * kvw), jnp.bfloat16)
    tall = jax.ShapeDtypeStruct((groups, 4 * rows, rows * width // (HD * groups)), jnp.bfloat16)
    return pl.pallas_call(
        attend_kernel,
        out_shape=[jax.ShapeDtypeStruct((rows, width), jnp.bfloat16), kept, share, share, share, tall, tall],
        in_specs=[SMEM] + [VMEM] * 13,
        out_specs=[VMEM] * 7,
        scratch_shapes=[
            pltpu.VMEM((rows, width), jnp.float32),
            pltpu.VMEM((rows, HD), jnp.float32),
            pltpu.VMEM((groups, rows, HD), jnp.float32),
            pltpu.VMEM((groups, rows, HD), jnp.float32),
            pltpu.VMEM((rows, 2 * kvw), jnp.bfloat16),
            pltpu.VMEM((groups, HD, rows), jnp.bfloat16),
        ]
        + [pltpu.VMEM((rows, 2 * rows), jnp.bfloat16)] * 4,
        compiler_params=params(VM_ATTEND),
        cost_estimate=cost(12.0),
    )(info, stream, cot, gain, queries, inverse, key_cols, *locals_, even_block, odd_block)


def terms_kernel(partner_count, info, cot, queries, low_all, grad_all, *outs):
    own_g, near_g, far_g = outs[:3]
    partners_g = outs[3 : 3 + partner_count]
    term = outs[3 + partner_count]
    rows, width = cot.shape
    groups = low_all.shape[0]
    kvw = groups * HD
    each = width // groups // HD
    factor = HD**-0.5
    me, want = info[0], info[2]
    odd = me % 2
    near_at = pl.multiple_of((1 - odd) * 2 * rows, rows)
    far_at = pl.multiple_of(odd * 2 * rows, rows)
    for g in range(groups):
        for part, (weights, ref, base) in enumerate(((grad_all, queries, 0), (low_all, cot, kvw))):
            heads = [ref[:, (g * each + h) * HD : (g * each + h + 1) * HD] for h in range(each)]
            n = 2 * g + part
            cols = slice(base + g * HD, base + (g + 1) * HD)
            sums = dot(weights[g], jnp.concatenate(heads, axis=0), NN)
            term[n] = sums * factor if part == 0 else sums
            own_g[:, cols] = term[n, rows : 2 * rows]
            near_g[:, cols] = term[n, pl.ds(near_at, rows)].astype(jnp.bfloat16)
            far_g[:, cols] = term[n, pl.ds(far_at, rows)].astype(jnp.bfloat16)
            picked = term[n, 3 * rows : 4 * rows].astype(jnp.bfloat16)
            for b in range(partner_count):
                hit = want == (me ^ (2 << b))
                partners_g[b][:, cols] = jnp.where(hit, picked, jnp.zeros_like(picked))


def terms_of(info, cot, queries, low_all, grad_all, partner_count):
    rows = cot.shape[0]
    groups = low_all.shape[0]
    kvw = groups * HD
    low = jax.ShapeDtypeStruct((rows, 2 * kvw), jnp.bfloat16)
    wide = jax.ShapeDtypeStruct((rows, 2 * kvw), jnp.float32)
    return pl.pallas_call(
        functools.partial(terms_kernel, partner_count),
        out_shape=[wide, low, low] + [low] * partner_count,
        in_specs=[SMEM] + [VMEM] * 4,
        out_specs=[VMEM] * (3 + partner_count),
        scratch_shapes=[pltpu.VMEM((2 * groups, 4 * rows, HD), jnp.float32)],
        compiler_params=params(VM_TERMS),
        cost_estimate=cost(5.0),
    )(info, cot, queries, low_all, grad_all)


def collect_kernel(own, *rest):
    total = own[...]
    for ref in rest[:-1]:
        total = total + ref[...].astype(jnp.float32)
    rest[-1][...] = total


def collect(own, parts):
    return pl.pallas_call(
        collect_kernel,
        out_shape=jax.ShapeDtypeStruct(own.shape, jnp.float32),
        in_specs=[VMEM] * (1 + len(parts)),
        out_specs=VMEM,
        compiler_params=params(VM_SMALL),
        cost_estimate=cost(0.5),
    )(own, *parts)


def finish_kernel(part_count, info, received, own, acc, *rest):
    previous, keys, values = rest[-3:]
    parts = rest[:part_count]
    terms = rest[part_count:-6]
    others = rest[-6:-3]
    previous[...] = received[...]
    kvw = keys.shape[1]
    rows = acc.shape[0]
    first = info[0] == 0
    last = acc[...]
    for ref in terms:
        last = last + ref[...].astype(jnp.float32)
    for k in range(4):
        at = slice(k * rows, (k + 1) * rows)
        total = own[at, :]
        for ref in parts:
            total = total + ref[at, :].astype(jnp.float32)
        part = last if k == 0 else others[k - 1][...].astype(jnp.float32)
        result = (total + jnp.where(first, part, 0.0)).astype(jnp.bfloat16)
        keys[at, :] = result[:, :kvw]
        values[at, :] = result[:, kvw:]


def finish(info, received, own, parts, acc, terms, others):
    shape = jax.ShapeDtypeStruct((own.shape[0], own.shape[1] // 2), jnp.bfloat16)
    return pl.pallas_call(
        functools.partial(finish_kernel, len(parts)),
        out_shape=[jax.ShapeDtypeStruct(received.shape, received.dtype), shape, shape],
        in_specs=[SMEM] + [VMEM] * (3 + len(parts) + len(terms) + len(others)),
        out_specs=[VMEM] * 3,
        compiler_params=params(VM_SMALL),
        cost_estimate=cost(0.5),
    )(info, received, own, acc, *parts, *terms, *others)


def permuted(value, pairs, axis="seq"):
    return lax.ppermute(value, axis, pairs)


def global_rounds(count, have):
    missing = [i for i in range(0, count, 2) if i not in have]
    rounds = []
    while missing:
        pairs = []
        for source in sorted(have, reverse=True):
            free = [t for t in missing if t not in [p[1] for p in pairs]]
            if free:
                best = min(free, key=lambda t: (bin(t ^ source).count("1"), abs(t - source)))
                pairs.append((source, best))
        rounds.append(pairs)
        have = have + [t for _, t in pairs]
        missing = [i for i in missing if i not in have]
    return rounds


def among(device, members):
    hit = device == members[0]
    for member in members[1:]:
        hit = hit | (device == member)
    return hit


def on_device(stream, cotangent, keys, values, gain, rand_blocks):
    hidden = stream[0]
    upstream = cotangent[0]
    count = lax.axis_size("seq")
    bits = count.bit_length() - 1
    device = lax.axis_index("seq")
    own = jnp.concatenate([keys[0], values[0]], axis=1)
    swaps = [[(i, i ^ (1 << b)) for i in range(count)] for b in range(bits)]
    across = [(i, i + 1) for i in range(1, count - 1, 2)]
    across = across + [(j, i) for i, j in across]
    info = jnp.stack([device, jnp.int32(count), rand_blocks[0, 0]])

    top = count // 4 * 3
    partners = [None] * bits
    for b in reversed(range(2, bits)):
        partners[b] = permuted(own, swaps[b])
    block_top = permuted(own, [(0, top)])
    partners[1] = permuted(own, swaps[1])
    far = permuted(own, across)
    near = permuted(own, swaps[0])

    block0 = jnp.where(device == top, block_top, own)
    for b in range(1, bits):
        block0 = jnp.where(device == (1 << b), partners[b], block0)
    kept, near = lax.optimization_barrier((gain, near))
    queries, inverse = norm(hidden, kept)
    block0, far, inverse = lax.optimization_barrier((block0, far, inverse))
    for pairs in global_rounds(count, [0, top] + [1 << b for b in range(1, bits)]):
        masks = {i ^ j for i, j in pairs}
        if len(masks) == 1:
            route = swaps[masks.pop().bit_length() - 1]
        else:
            route = pairs
        moved = permuted(block0, route)
        block0 = jnp.where(among(device, [t for _, t in pairs]), moved, block0)
    slots, key_cols = arrange(info, own, near, far, partners[1:])
    locals_ = list(local(info, upstream, queries, slots))
    block0, locals_[2] = lax.optimization_barrier((block0, locals_[2]))
    odd_block = permuted(block0, swaps[0])
    handed, keep_g, beside_g, across_g, corner_g, low_all, grad_all = attend(
        info, hidden, upstream, gain, queries, inverse, key_cols, locals_, block0, odd_block
    )
    outs = terms_of(info, upstream, queries, low_all, grad_all, bits - 1)
    own_g, near_g, far_g = outs[:3]
    partners_g = outs[3:]

    sections = lax.axis_size("section")
    back = [((i + 1) % sections, i) for i in range(sections)]
    rows = own.shape[0]

    def swapped(value, mask):
        return permuted(value, [(i, i ^ mask) for i in range(count)])

    received = permuted(handed, back, "section")
    near_r = permuted(near_g, swaps[0])
    y_r = permuted(partners_g[0], swaps[1])
    far_r = permuted(far_g, across)
    z_r = [permuted(partners_g[b - 1], swaps[b]) for b in range(2, bits)]

    terms = [swapped(beside_g, 1), swapped(across_g, 2), swapped(corner_g, 3)]
    acc = keep_g
    for b in range(2, bits, 2):
        acc = acc + sum(t.astype(jnp.float32) for t in terms)
        low = acc.astype(jnp.bfloat16)
        terms = [swapped(low, k << b) for k in range(1, 1 << min(2, bits - b))]
    mine = (acc + sum(t.astype(jnp.float32) for t in terms)).astype(jnp.bfloat16)
    others = [swapped(mine, mask) for mask in (1, 2, 3)]
    own_g = collect(own_g, [y_r] + z_r)
    parts = [near_r, far_r]
    previous, key_grads, value_grads = finish(info, received, own_g, parts, acc, terms, others)
    return (previous[None], key_grads[None], value_grads[None])


def solution(mesh):
    return jax.shard_map(
        on_device,
        mesh=mesh,
        in_specs=(
            P("section", "seq", None),
            P("section", "seq", None),
            P("section", "seq", None),
            P("section", "seq", None),
            P("section", None),
            P("seq", None),
        ),
        out_specs=(P("section", "seq", None), P("section", "seq", None), P("section", "seq", None)),
        check_vma=False,
    )
```
